128 devices in a mesh: fsdp: 4 (over y), dp: 16 (over z_lo, x, core), owner: 2 (over z_hi).
Axes of the slice: x: 4, y: 4, z: 4 (z_hi: 2, z_lo: 2; z = z_hi * 2 + z_lo), core: 2. Of those that a mesh axis runs over, the one named last changes fastest.
Arguments:
- tokens: bfloat16 [65536, 4608], P(('fsdp', 'dp', 'owner')), may hold values from -6 to 6
- output_gradient: bfloat16 [65536, 2048], P(('fsdp', 'dp', 'owner')), may hold values from -6 to 6
- tile_language: int32 [512], replicated, may hold values from 0 to 63, as said below
- tile_live_count: int32 [512], replicated, may hold values from 1 to 128, as said below
- frozen_weight: bfloat16 [4608, 2048], P('fsdp'), may hold values from -0.09375 to 0.09375
- adapter_down: bfloat16 [64, 32, 4608], P('owner', None, 'fsdp'), may hold values from -0.09375 to 0.09375
- adapter_up: bfloat16 [64, 32, 2048], P('owner', None, 'fsdp'), may hold values from -1 to 1
Outputs:
- input_gradient: bfloat16 [65536, 4608], P(('fsdp', 'dp', 'owner'))
- grad_down: bfloat16 [64, 32, 4608], P('owner', None, 'fsdp')
- grad_up: bfloat16 [64, 32, 2048], P('owner', None, 'fsdp')
The draws below stay inside these ranges and needn't reach their ends.
Inputs may be any that keep to these rules, and one draw needn't show every extreme that they name: `tile_language`: the tiles of the device with fsdp index f, dp index e and owner index o are tiles ((f * 16 + e) * 2 + o) * 4 onward; all of them name languages o * 32 to (o + 1) * 32 - 1. `tile_live_count`: the live slots of a tile are its first ones.
All inputs are finite; a program needn't handle non-finite values.
Results may differ from the reference program's by a relative error of at most 0.0051.
Values may be sent and summed in bfloat16 or wider, within the bound.
A program may use at most 128 MiB of HBM per device.

```python
import jax
import jax.numpy as jnp

MODEL_WIDTH = 4608
QUERY_WIDTH = 2048
ADAPTER_RANK = 32
LANGUAGE_COUNT = 64
TILE_TOKENS = 128
TOK_DEV = 512
TOKEN_SLOTS = 65536
N_OWNER = 2


def draw_tile_language(key, part):
    key = jax.random.fold_in(key, 11)
    first, second, third, fourth = jax.random.split(key, 4)
    tiles_dev = TOK_DEV // TILE_TOKENS
    language_owner = LANGUAGE_COUNT // N_OWNER
    count = TOKEN_SLOTS // TILE_TOKENS
    pick = jnp.minimum(jax.random.randint(first, (count,), 0, language_owner), jax.random.randint(second, (count,), 0, language_owner))
    pick = jnp.minimum(pick, jax.random.randint(third, (count,), 0, language_owner))
    order = jax.random.permutation(fourth, language_owner).astype(jnp.int32)
    device = jnp.arange(count, dtype=jnp.int32) // tiles_dev
    owner = device % N_OWNER
    langs = owner * language_owner + jnp.take(order, pick)
    position = jnp.arange(count, dtype=jnp.int32)
    langs = jnp.where(position == 0, 0, langs)
    langs = jnp.where(position == tiles_dev, LANGUAGE_COUNT - 1, langs)
    return langs.astype(jnp.int32)


def draw_tile_live_count(key, part):
    key = jax.random.fold_in(key, 23)
    count = TOKEN_SLOTS // TILE_TOKENS
    fills = jax.random.randint(key, (count,), 1, TILE_TOKENS + 1)
    position = jnp.arange(count, dtype=jnp.int32)
    fills = jnp.where(position == 0, TILE_TOKENS, fills)
    fills = jnp.where(position == 1, 1, fills)
    return fills.astype(jnp.int32)


def levels(own_key, dims, pieces, least, high):
    factor_of, own = 1.0, jax.random.fold_in(own_key, 6)
    for dim, parts in pieces:
        draws = jnp.exp(jax.random.uniform(jax.random.fold_in(own, dim), (parts,), jnp.float32, least / len(pieces), high / len(pieces)))
        factor_of = factor_of * jnp.repeat(draws, dims[dim] // parts).reshape([-1 if axis == dim else 1 for axis in range(len(dims))])
    return factor_of


def bell_draw(key, dims, scale, reach, cuts=(), held_as=jnp.bfloat16):
    entries = scale * jax.random.normal(key, dims, jnp.float32)
    if cuts:
        entries = entries * levels(key, dims, cuts, -0.22, 0.18)
    return jnp.clip(entries, -reach, reach).astype(held_as)


def setup_inputs(seed: int = 0) -> dict:
    arg_keys = jax.random.split(jax.random.key(seed), 8)
    tokens = bell_draw(arg_keys[0], (TOKEN_SLOTS, MODEL_WIDTH), 1.0, 6.0, ((0, 128),))
    output_gradient = bell_draw(arg_keys[1], (TOKEN_SLOTS, QUERY_WIDTH), 1.0, 6.0, ((0, 128),))
    tile_language = draw_tile_language(jax.random.fold_in(arg_keys[7], 71), 0)
    tile_live_count = draw_tile_live_count(jax.random.fold_in(arg_keys[7], 71), 0)
    frozen_weight = bell_draw(arg_keys[4], (MODEL_WIDTH, QUERY_WIDTH), MODEL_WIDTH ** -0.5, 0.09375, ((0, 4),))
    adapter_down = bell_draw(arg_keys[5], (LANGUAGE_COUNT, ADAPTER_RANK, MODEL_WIDTH), MODEL_WIDTH ** -0.5, 0.09375, ((0, 2), (2, 4)))
    adapter_up = bell_draw(arg_keys[6], (LANGUAGE_COUNT, ADAPTER_RANK, QUERY_WIDTH), ADAPTER_RANK ** -0.5, 1.0, ((0, 2), (2, 4)))
    return dict(tokens=tokens, output_gradient=output_gradient, tile_language=tile_language, tile_live_count=tile_live_count, frozen_weight=frozen_weight, adapter_down=adapter_down, adapter_up=adapter_up)


adapter_scale = 2.0


def reference(tokens, output_gradient, tile_language, tile_live_count, frozen_weight, adapter_down, adapter_up):
    tiles = TOKEN_SLOTS // TILE_TOKENS
    tok_tiles = tokens.reshape(tiles, TILE_TOKENS, MODEL_WIDTH).astype(jnp.float32)
    gradient_tiles = output_gradient.reshape(tiles, TILE_TOKENS, QUERY_WIDTH).astype(jnp.float32)
    live_mask = (jnp.arange(TILE_TOKENS, dtype=jnp.int32)[None, :] < tile_live_count[:, None])[:, :, None]
    selected_down = jnp.take(adapter_down, tile_language, axis=0).astype(jnp.float32)
    selected_up = jnp.take(adapter_up, tile_language, axis=0).astype(jnp.float32)
    hidden_state = jnp.where(live_mask, jnp.einsum("ktd,krd->ktr", tok_tiles, selected_down), 0.0).astype(jnp.bfloat16)
    backward_input = jnp.where(live_mask, jnp.einsum("bca,bea->bce", gradient_tiles, selected_up), 0.0).astype(jnp.bfloat16)
    frozen_output = jnp.dot(output_gradient, frozen_weight.T, preferred_element_type=jnp.float32).reshape(tiles, TILE_TOKENS, MODEL_WIDTH)
    adapter_extra = jnp.einsum("ktr,krd->ktd", backward_input.astype(jnp.float32), selected_down)
    input_gradient = jnp.where(live_mask, frozen_output + adapter_scale * adapter_extra, 0.0).astype(jnp.bfloat16).reshape(TOKEN_SLOTS, MODEL_WIDTH)
    adapter_factor = adapter_scale * float(TOKEN_SLOTS) ** -0.5
    part_down = jnp.einsum("ktr,ktd->krd", backward_input.astype(jnp.float32), tok_tiles)
    partial_up = jnp.einsum("sow,soz->swz", hidden_state.astype(jnp.float32), gradient_tiles)
    grad_down = (jax.ops.segment_sum(part_down, tile_language, num_segments=LANGUAGE_COUNT) * adapter_factor).astype(jnp.bfloat16)
    grad_up = (jax.ops.segment_sum(partial_up, tile_language, num_segments=LANGUAGE_COUNT) * adapter_factor).astype(jnp.bfloat16)
    return input_gradient, grad_down, grad_up
```

```python
import functools

import jax
import jax.numpy as jnp
from jax import lax
from jax.experimental import pallas as pl
from jax.experimental.pallas import tpu as pltpu
from jax.sharding import PartitionSpec as P

MESH = pl.DeviceIdType.MESH
NT = (((1,), (1,)), ((), ()))
NN = (((1,), (0,)), ((), ()))

TILE = 128
TILES = 4
RANK = 32
ROWS = TILES * RANK
LANGS = 32
YN = 4
CHIPS = 8
DP = 16
T = TILE * TILES
D_ALL, Q_ALL = 4608, 2048
D_SH, Q_SH = D_ALL // YN, Q_ALL // YN
SUB = 32
BLK = 4 * SUB
HALF = 4 * BLK
TAIL = D_SH - 2 * HALF


def dot(a, b, dims=NN):
    return lax.dot_general(a, b, dims, preferred_element_type=jnp.float32)


def permutation(shape):
    i = lax.broadcasted_iota(jnp.int32, shape, 0)
    j = lax.broadcasted_iota(jnp.int32, shape, 1)
    k, q, r = lax.div(lax.rem(j, 16), 4), lax.div(j, 16), lax.rem(j, 4)
    return (i == k * RANK + q * 4 + r).astype(jnp.float32).astype(jnp.bfloat16)


def main_kernel(
    lang, live, lang_cols, tokens, grad, weight, adown, aup,
    ig, gd, gu,
    wbuf, wtail, wl, tok, og, adv, auv, su, sd, uu, dd, spd, spu, r1d, r1u, r2d, r2u, gdv, guv, igv, b2, btp, htp,
    in_sem, y_s, y_r, a_s, a_r, b_s, b_r, f_s, f_r, c_s, c_r, t_s, t_r, tc_s, tc_r,
    u_s, u_r, d_s, d_r, pd_s, pd_r, pu_s, pu_r, xd_s, xd_r, xu_s, xu_r, ag_s, ag_r, agc_s, agc_r, own_s, out_s,
):
    f, e, o = lax.axis_index("fsdp"), lax.axis_index("dp"), lax.axis_index("owner")
    q, c = lax.div(e, 2), lax.rem(e, 2)
    x, z = lax.rem(q, 4), o * 2 + lax.div(q, 4)
    pa = x * (1 - c) + z * c
    pb = z * (1 - c) + x * c

    def mod(v, n):
        return lax.rem(v + n, n)

    def at_ab(da, db):
        a, b = mod(pa + da, 4), mod(pb + db, 4)
        xx, zz = a * (1 - c) + b * c, b * (1 - c) + a * c
        return (f, lax.rem(zz, 2) * 8 + xx * 2 + c, lax.div(zz, 2))

    def at_y(s):
        return (mod(f + s, 4), e, o)

    def at_dp(chip, core):
        return (f, chip * 2 + core, o)

    other = at_dp(q, 1 - c)

    def rcopy(src, dst, ssem, rsem, dev):
        return pltpu.make_async_remote_copy(
            src_ref=src, dst_ref=dst, send_sem=ssem, recv_sem=rsem, device_id=dev, device_id_type=MESH
        )

    def await_ref(ref, sem):
        pltpu.make_async_copy(ref, ref, sem).wait()

    sends = []

    def send(*args):
        cp = rcopy(*args)
        cp.start()
        sends.append(cp)

    loads = [
        pltpu.make_async_copy(s, d, in_sem.at[i])
        for i, (s, d) in enumerate(((aup, auv), (adown, adv), (grad, og), (tokens, tok), (weight, wl)))
    ]
    for cp in loads:
        cp.start()

    barrier = pltpu.get_barrier_semaphore()
    peers = [at_y(s) for s in (1, 2, 3)]
    peers += [at_ab(s, 0) for s in (1, 2, 3)] + [at_ab(0, 1), at_ab(0, -1)]
    peers += [(f, mod(e + s, DP), o) for s in range(1, DP)]
    for dev in peers:
        pl.semaphore_signal(barrier, inc=1, device_id=dev, device_id_type=MESH)
    pl.semaphore_wait(barrier, len(peers))

    sub0 = pl.multiple_of(pa * SUB, SUB)
    piece = pl.multiple_of(c * HALF + pb * BLK + pa * SUB, SUB)
    for s in (2, 1, 3):
        send(
            weight.at[pl.ds(piece, SUB)], wbuf.at[3 - s, 0, c, pl.ds(sub0, SUB)],
            y_s.at[s - 1], y_r.at[3 - s], at_y(s),
        )

    def choose(table, s, out):
        first = ((mod(f + s, 4) * DP + e) * 2 + o) * TILES
        for k in range(TILES):
            out[pl.ds(k * RANK, RANK), :] = table[lax.rem(lang[first + k], LANGS)]

    loads[0].wait()
    for s in (2, 1, 3):
        choose(auv, s, su.at[s - 1])
        send(su.at[s - 1], uu.at[f], u_s.at[s - 1], u_r.at[s - 1], at_y(s))
    choose(auv, 0, uu.at[f])
    loads[1].wait()
    for s in (2, 1, 3):
        choose(adv, s, sd.at[s - 1])
        send(sd.at[s - 1], dd.at[f], d_s.at[s - 1], d_r.at[s - 1], at_y(s))
    choose(adv, 0, dd.at[f])

    loads[2].wait()
    own = ((f * DP + e) * 2 + o) * TILES
    slot = lax.broadcasted_iota(jnp.int32, (TILE, Q_ALL), 0)
    for k in range(TILES):
        rows = pl.ds(k * TILE, TILE)
        og[rows, :] = jnp.where(slot < live[own + k], og[rows, :].astype(jnp.float32), 0.0).astype(jnp.bfloat16)

    def b_sends(s):
        rows = pl.ds(pl.multiple_of(mod(pa - s, 4) * SUB, SUB), SUB)
        unit = wbuf.at[:, 0, c, rows]
        send(unit, wbuf.at[:, 3, c, rows], b_s.at[0, s], b_r.at[0, s], at_ab(0, 1))
        send(unit, wbuf.at[:, 1, c, rows], b_s.at[1, s], b_r.at[1, s], at_ab(0, -1))

    for i in range(3):
        await_ref(wbuf.at[i, 0, c, pl.ds(sub0, SUB)], y_r.at[i])
    own_unit = wbuf.at[:, 0, c, pl.ds(sub0, SUB)]
    for s in (2, 1, 3):
        send(own_unit, own_unit, a_s.at[s - 1], a_r.at[s - 1], at_ab(s, 0))
    b_sends(0)

    for s in (1, 3, 2):
        await_ref(uu.at[mod(f - s, 4)], u_r.at[s - 1])
    j = lax.broadcasted_iota(jnp.int32, (ROWS, T), 0)
    t = lax.broadcasted_iota(jnp.int32, (ROWS, T), 1)
    limit = jnp.where(
        t < 2 * TILE,
        jnp.where(t < TILE, live[own], live[own + 1]),
        jnp.where(t < 3 * TILE, live[own + 2], live[own + 3]),
    )
    mask = (lax.div(j, RANK) == lax.div(t, TILE)) & (lax.rem(t, TILE) < limit)
    perm_t = permutation((ROWS, ROWS)).astype(jnp.float32).T.astype(jnp.bfloat16)

    def rows_by_chip(v):
        v = jnp.where(mask, v, 0.0).astype(jnp.bfloat16)
        return dot(perm_t, v).astype(jnp.bfloat16)

    bt = jnp.zeros((ROWS, T), jnp.float32)
    bb = jnp.zeros((T, ROWS), jnp.float32)
    for y in range(YN):
        bt += dot(uu[y], og[:, y * Q_SH : (y + 1) * Q_SH], NT)
        bb += dot(og[:, y * Q_SH : (y + 1) * Q_SH], uu[y], NT)
    tt = lax.broadcasted_iota(jnp.int32, (T, ROWS), 0)
    jj = lax.broadcasted_iota(jnp.int32, (T, ROWS), 1)
    bb = jnp.where(lax.div(jj, RANK) == lax.div(tt, TILE), bb, 0.0).astype(jnp.bfloat16)
    b2[...] = (bb.astype(jnp.float32) * 2.0).astype(jnp.bfloat16)
    btp[...] = rows_by_chip(bt)

    loads[3].wait()
    for s in (2, 1, 3, 0):
        y = mod(f + s, 4)
        part = dot(btp[...], tok[:, pl.ds(pl.multiple_of(y * D_SH, TILE), D_SH)]).astype(jnp.bfloat16)
        if s:
            spd[s - 1] = part
            send(spd.at[s - 1], r1d.at[f], pd_s.at[s - 1], pd_r.at[s - 1], at_y(s))
        else:
            r1d[f] = part

    def spread(core, r1, r2, s, ssem, rsem):
        y = mod(f - s, 4)

        def one(i, _):
            chip = lax.rem(q + i, CHIPS)
            src = r1.at[y, pl.ds(pl.multiple_of(chip * 16, 16), 16)]

            @pl.when((i > 0) | (c != core))
            def _():
                rcopy(src, r2.at[e, y], ssem.at[s, i], rsem, at_dp(chip, core)).start()

            @pl.when((i == 0) & (c == core))
            def _():
                pltpu.make_async_copy(src, r2.at[e, y], rsem).start()

            return 0

        lax.fori_loop(0, CHIPS, one, 0)

    def spread_done(core, r1, r2, ssem):
        def one(i, _):
            s, t = lax.div(i, CHIPS), lax.rem(i, CHIPS)

            @pl.when((t > 0) | (c != core))
            def _():
                src = r1.at[0, pl.ds(0, 16)]
                rcopy(src, r2.at[0, 0], ssem.at[s, t], ssem.at[s, t], at_dp(q, 1 - c)).wait_send()

            return 0

        lax.fori_loop(0, YN * CHIPS, one, 0)

    spread(0, r1d, r2d, 0, xd_s, xd_r.at[0])

    def columns(w, y, first, width):
        d = dd[y, :, pl.ds(first, width)]
        return (dot(og[...], w, NT) + dot(b2[...], d)).astype(jnp.bfloat16)

    def put(y, first, width, value):
        igv[:, pl.ds(pl.multiple_of(y * D_SH + first, TILE), width)] = value

    loads[4].wait()

    def local_chunk(i, _):
        first = pl.multiple_of(i * 384, TILE)
        put(f, first, 384, columns(wl[pl.ds(first, 384), :], f, first, 384))
        return 0

    lax.fori_loop(0, D_SH // 384, local_chunk, 0)

    for s in (1, 3, 2):
        rows = pl.ds(pl.multiple_of(mod(pa - s, 4) * SUB, SUB), SUB)
        await_ref(wbuf.at[:, 0, c, rows], a_r.at[s - 1])
        b_sends(s)

    def to_other(rel):
        send(wbuf.at[:, rel, c], wbuf.at[:, rel, c], c_s.at[rel], c_r.at[rel], other)

    to_other(0)

    def pass_on(s):
        rows = pl.ds(pl.multiple_of(mod(pa - s, 4) * SUB, SUB), SUB)
        await_ref(wbuf.at[:, 3, c, rows], b_r.at[0, s])
        await_ref(wbuf.at[:, 1, c, rows], b_r.at[1, s])
        if s in (0, 2):
            send(wbuf.at[:, 3, c, rows], wbuf.at[:, 2, c, rows], f_s.at[s], f_r.at[s], at_ab(0, 1))
        else:
            send(wbuf.at[:, 1, c, rows], wbuf.at[:, 2, c, rows], f_s.at[s], f_r.at[s], at_ab(0, -1))

    pass_on(0)

    for s in (1, 3, 2):
        await_ref(dd.at[mod(f - s, 4)], d_r.at[s - 1])
    ht = jnp.zeros((ROWS, T), jnp.float32)
    for y in range(YN):
        ht += dot(dd[y], tok[:, y * D_SH : (y + 1) * D_SH], NT)
    htp[...] = rows_by_chip(ht)
    for s in (2, 1, 3, 0):
        y = mod(f + s, 4)
        part = dot(htp[...], og[:, pl.ds(pl.multiple_of(y * Q_SH, TILE), Q_SH)]).astype(jnp.bfloat16)
        if s:
            spu[s - 1] = part
            send(spu.at[s - 1], r1u.at[f], pu_s.at[s - 1], pu_r.at[s - 1], at_y(s))
        else:
            r1u[f] = part
    spread(1, r1u, r2u, 0, xu_s, xu_r.at[0])

    mine = pl.ds(pl.multiple_of(c * (TAIL // 2), TAIL // 2), TAIL // 2)
    tail_rows = pl.ds(pl.multiple_of(2 * HALF + c * (TAIL // 2), TAIL // 2), TAIL // 2)
    for s in (2, 1, 3):
        send(weight.at[tail_rows], wtail.at[3 - s, mine], t_s.at[s - 1], t_r.at[3 - s], at_y(s))

    for s in (1, 3, 2):
        pass_on(s)
    for rel in (1, 3):
        to_other(rel)

    for s in (1, 3, 2):
        await_ref(r1d.at[mod(f - s, 4)], pd_r.at[s - 1])
        spread(0, r1d, r2d, s, xd_s, xd_r.at[0])

    def block(rel):
        await_ref(wbuf.at[:, rel, 1 - c], c_r.at[rel])

        def one(i, _):
            y = mod(f + i + 1, 4)
            w = wbuf[i, rel].reshape(2 * BLK, Q_ALL)
            first0 = pl.multiple_of(mod(z + rel, 4) * BLK, BLK)
            first1 = pl.multiple_of(HALF + mod(x + rel, 4) * BLK, BLK)
            acc = dot(og[...], w, NT)
            add0 = dot(b2[...], dd[y, :, pl.ds(first0, BLK)])
            add1 = dot(b2[...], dd[y, :, pl.ds(first1, BLK)])
            put(y, first0, BLK, (acc[:, :BLK] + add0).astype(jnp.bfloat16))
            put(y, first1, BLK, (acc[:, BLK:] + add1).astype(jnp.bfloat16))
            return 0

        lax.fori_loop(0, 3, one, 0)

    block(0)

    for s in (1, 3, 2):
        await_ref(r1u.at[mod(f - s, 4)], pu_r.at[s - 1])
        spread(1, r1u, r2u, s, xu_s, xu_r.at[0])

    block(1)
    block(3)

    def add_up(r2, rsem, gv, g):
        await_ref(r2, rsem)
        m = lax.broadcasted_iota(jnp.int32, (CHIPS * 16, DP * YN * 16), 0)
        n = lax.broadcasted_iota(jnp.int32, (CHIPS * 16, DP * YN * 16), 1)
        hit = (lang_cols[o] - o * LANGS == lax.div(m, 4)) & (lax.rem(n, 4) == lax.rem(m, 4))
        pick = hit.astype(jnp.float32).astype(jnp.bfloat16)
        width = r2.shape[-1]
        total = dot(pick, r2[...].reshape(DP * YN * 16, width))
        gv[...] = (total * (2.0 / 256.0)).astype(jnp.bfloat16)
        for s in range(1, CHIPS):
            rcopy(gv, g.at[q], ag_s.at[s - 1], ag_r.at[s - 1], at_dp(mod(q + s, CHIPS), c)).start()
        rcopy(gv, g.at[q], agc_s.at[0], agc_r.at[0], other).start()
        pltpu.make_async_copy(gv, g.at[q], own_s.at[0]).start()

    def gather_up(gv, g):
        for s in range(1, CHIPS):
            part = g.at[mod(q - s, CHIPS)]
            await_ref(part, ag_r.at[s - 1])
            rcopy(part, part, agc_s.at[s], agc_r.at[s], other).start()
        await_ref(gv, own_s.at[0])
        for s in range(1, CHIPS):
            rcopy(gv, g.at[q], ag_s.at[s - 1], ag_r.at[s - 1], other).wait_send()
        for s in range(CHIPS):
            rcopy(gv, g.at[q], agc_s.at[s], agc_r.at[s], other).wait_send()

    def from_other(g):
        for s in range(CHIPS):
            await_ref(g.at[mod(q - s, CHIPS)], agc_r.at[s])

    @pl.when(c == 0)
    def _():
        add_up(r2d, xd_r.at[0], gdv, gd)

    for s in range(4):
        rows = pl.ds(pl.multiple_of(mod(pa - s, 4) * SUB, SUB), SUB)
        await_ref(wbuf.at[:, 2, c, rows], f_r.at[s])
    to_other(2)
    for i in range(3):
        await_ref(wtail.at[i, mine], t_r.at[i])
    send(wtail.at[:, mine], wtail.at[:, mine], tc_s.at[0], tc_r.at[0], other)

    @pl.when(c == 1)
    def _():
        add_up(r2u, xu_r.at[0], guv, gu)

    block(2)
    theirs = pl.ds(pl.multiple_of((1 - c) * (TAIL // 2), TAIL // 2), TAIL // 2)
    await_ref(wtail.at[:, theirs], tc_r.at[0])

    def tail_chunk(i, _):
        y = mod(f + i + 1, 4)
        put(y, 2 * HALF, TAIL, columns(wtail[i], y, 2 * HALF, TAIL))
        return 0

    lax.fori_loop(0, 3, tail_chunk, 0)
    out = pltpu.make_async_copy(igv, ig, out_s.at[0])
    out.start()

    @pl.when(c == 0)
    def _():
        gather_up(gdv, gd)
        from_other(gu)

    @pl.when(c == 1)
    def _():
        gather_up(guv, gu)
        from_other(gd)

    for cp in sends:
        cp.wait_send()
    spread_done(0, r1d, r2d, xd_s)
    spread_done(1, r1u, r2u, xu_s)
    out.wait()


def finish_kernel(gd, gu, ig_in, down, up, ig, sem):
    cp = pltpu.make_async_copy(ig_in, ig, sem)
    cp.start()
    perm = permutation((ROWS, ROWS))
    for src, dst in ((gd, down), (gu, up)):
        width = src.shape[-1]
        for g in range(CHIPS):
            rows = src[:, g * 16 : (g + 1) * 16, :].reshape(ROWS, width)
            dst[g * 4 : (g + 1) * 4] = dot(perm, rows).astype(jnp.bfloat16).reshape(4, RANK, width)
    cp.wait()


def on_device(tokens, output_gradient, tile_language, tile_live_count, frozen_weight, adapter_down, adapter_up):
    bf = jnp.bfloat16
    by_owner = tile_language.reshape(YN, DP, 2, TILES).transpose(2, 1, 0, 3)
    lang_cols = jnp.repeat(by_owner.reshape(2, 1, DP * YN * TILES), 4, axis=2)
    hbm, smem, vmem = (pl.BlockSpec(memory_space=s) for s in (pl.ANY, pltpu.SMEM, pltpu.VMEM))
    sem = pltpu.SemaphoreType.DMA

    def sems(*shapes):
        return [sem(s) for s in shapes]

    ig, gd, gu = pl.pallas_call(
        main_kernel,
        out_shape=(
            jax.ShapeDtypeStruct((T, D_ALL), bf),
            jax.ShapeDtypeStruct((CHIPS, CHIPS * 16, D_SH), bf),
            jax.ShapeDtypeStruct((CHIPS, CHIPS * 16, Q_SH), bf),
        ),
        in_specs=[smem, smem, vmem, hbm, hbm, hbm, hbm, hbm],
        out_specs=(hbm, hbm, hbm),
        scratch_shapes=[
            pltpu.VMEM((3, 4, 2, BLK, Q_ALL), bf),
            pltpu.VMEM((3, TAIL, Q_ALL), bf),
            pltpu.VMEM((D_SH, Q_ALL), bf),
            pltpu.VMEM((T, D_ALL), bf),
            pltpu.VMEM((T, Q_ALL), bf),
            pltpu.VMEM((LANGS, RANK, D_SH), bf),
            pltpu.VMEM((LANGS, RANK, Q_SH), bf),
            pltpu.VMEM((3, ROWS, Q_SH), bf),
            pltpu.VMEM((3, ROWS, D_SH), bf),
            pltpu.VMEM((YN, ROWS, Q_SH), bf),
            pltpu.VMEM((YN, ROWS, D_SH), bf),
            pltpu.VMEM((3, ROWS, D_SH), bf),
            pltpu.VMEM((3, ROWS, Q_SH), bf),
            pltpu.VMEM((YN, ROWS, D_SH), bf),
            pltpu.VMEM((YN, ROWS, Q_SH), bf),
            pltpu.VMEM((DP, YN, 16, D_SH), bf),
            pltpu.VMEM((DP, YN, 16, Q_SH), bf),
            pltpu.VMEM((CHIPS * 16, D_SH), bf),
            pltpu.VMEM((CHIPS * 16, Q_SH), bf),
            pltpu.VMEM((T, D_ALL), bf),
            pltpu.VMEM((T, ROWS), bf),
            pltpu.VMEM((ROWS, T), bf),
            pltpu.VMEM((ROWS, T), bf),
            *sems((5,), (3,), (3,), (3,), (3,), (2, 4), (2, 4), (4,), (4,), (4,), (4,), (3,), (3,), (1,), (1,)),
            *sems((3,), (3,), (3,), (3,), (3,), (3,), (3,), (3,), (4, 8), (1,), (4, 8), (1,)),
            *sems((7,), (7,), (8,), (8,), (1,), (1,)),
        ],
        compiler_params=pltpu.CompilerParams(
            collective_id=0, has_side_effects=True, vmem_limit_bytes=58 * 2**20
        ),
        cost_estimate=pl.CostEstimate(flops=12 * 10**9, bytes_accessed=40 * 10**6, transcendentals=0),
        name="exchange",
    )(tile_language, tile_live_count, lang_cols, tokens, output_gradient, frozen_weight, adapter_down, adapter_up)
    down, up, ig = pl.pallas_call(
        finish_kernel,
        out_shape=(
            jax.ShapeDtypeStruct((LANGS, RANK, D_SH), bf),
            jax.ShapeDtypeStruct((LANGS, RANK, Q_SH), bf),
            jax.ShapeDtypeStruct((T, D_ALL), bf),
        ),
        in_specs=[vmem, vmem, hbm],
        out_specs=(vmem, vmem, hbm),
        scratch_shapes=[sem],
        compiler_params=pltpu.CompilerParams(vmem_limit_bytes=40 * 2**20),
        name="finish",
    )(gd, gu, ig)
    return ig, down, up


def solution(mesh):
    tok = P(("fsdp", "dp", "owner"), None)
    adapter = P("owner", None, "fsdp")
    return jax.shard_map(
        on_device,
        mesh=mesh,
        in_specs=(tok, tok, P(), P(), P("fsdp", None), adapter, adapter),
        out_specs=(tok, adapter, adapter),
        check_vma=False,
    )
```

```python
import functools

import jax
import jax.numpy as jnp
from jax import lax
from jax.experimental import pallas as pl
from jax.experimental.pallas import tpu as pltpu
from jax.sharding import PartitionSpec as P

MESH = pl.DeviceIdType.MESH
NT = (((1,), (1,)), ((), ()))
NN = (((1,), (0,)), ((), ()))

TILE = 128
TILES = 4
RANK = 32
ROWS = TILES * RANK
LANGS = 32
YN = 4
CHIPS = 8
T = TILE * TILES
D_ALL, Q_ALL = 4608, 2048
D_SH, Q_SH = D_ALL // YN, Q_ALL // YN
G_ALL = D_SH + Q_SH
CUT = 896
SUB = 112
HALF = 4 * SUB
TAIL = D_SH - 2 * HALF
MINE = TAIL // 2
LOCAL = 384
SLOTS = (1, 3, 2)
SLOT_OF = {1: 0, 3: 1, 2: 2}


def dot(a, b, dims=NN):
    return lax.dot_general(a, b, dims, preferred_element_type=jnp.float32)


def one_hot(cond):
    return cond.astype(jnp.float32).astype(jnp.bfloat16)


def iota(shape, dim):
    return lax.broadcasted_iota(jnp.int32, shape, dim)


def permutation(shape):
    i, j = iota(shape, 0), iota(shape, 1)
    k, q, r = lax.div(lax.rem(j, 16), 4), lax.div(j, 16), lax.rem(j, 4)
    return one_hot(i == k * RANK + q * 4 + r)


def main_kernel(
    lang, live, lang_row, tokens, grad, weight, adown, aup,
    ig, gg,
    wbuf, wl, tok, og, adv, auv, su, sd, uu, dd, spd, spu, r1d, r1u, r2d, r2u, xout, xin, gv, igv, b2, btp, htp, pick,
    in_sem, y_s, y_r, a_s, a_r, b_s, b_r, f_s, f_r, c_s, c_r, t_s, t_r, tf_s, tf_r, tc_s, tc_r,
    u_s, u_r, d_s, d_r, pd_s, pd_r, pu_s, pu_r, xd_s, xd_r, xu_s, xu_r, xc_s, xc_r, g_s, g_r, e_s, e_r, own_s, out_s,
):
    f, e, o = lax.axis_index("fsdp"), lax.axis_index("dp"), lax.axis_index("owner")
    q, c = lax.div(e, 2), lax.rem(e, 2)
    x, zl = lax.rem(q, 4), lax.div(q, 4)
    z = o * 2 + zl
    pa = x * (1 - c) + z * c
    pb = z * (1 - c) + x * c

    def mod(v, n):
        return lax.rem(v + n, n)

    def at_ab(da, db):
        a, b = mod(pa + da, 4), mod(pb + db, 4)
        xx, zz = a * (1 - c) + b * c, b * (1 - c) + a * c
        return (f, lax.rem(zz, 2) * 8 + xx * 2 + c, lax.div(zz, 2))

    def at_y(s):
        return (mod(f + s, 4), e, o)

    def at_chip(chip):
        return (f, chip * 2 + c, o)

    def chip_of(dz, s):
        return lax.rem(zl + dz, 2) * 4 + mod(x - s, 4)

    other = (f, q * 2 + 1 - c, o)

    def rcopy(src, dst, ssem, rsem, dev):
        return pltpu.make_async_remote_copy(
            src_ref=src, dst_ref=dst, send_sem=ssem, recv_sem=rsem, device_id=dev, device_id_type=MESH
        )

    def await_ref(ref, sem):
        pltpu.make_async_copy(ref, ref, sem).wait()

    sends = []

    def send(*args):
        cp = rcopy(*args)
        cp.start()
        sends.append(cp)

    loads = [
        pltpu.make_async_copy(s, d, in_sem.at[i])
        for i, (s, d) in enumerate(((aup, auv), (adown, adv), (grad, og), (tokens, tok), (weight, wl)))
    ]
    for cp in loads:
        cp.start()

    barrier = pltpu.get_barrier_semaphore()
    peers = [at_y(s) for s in (1, 2, 3)]
    peers += [at_ab(s, 0) for s in (1, 2, 3)] + [at_ab(0, 1), at_ab(0, -1)]
    peers += [at_chip(lax.rem(q + s, CHIPS)) for s in range(1, CHIPS)] + [other]
    for dev in peers:
        pl.semaphore_signal(barrier, inc=1, device_id=dev, device_id_type=MESH)
    pl.semaphore_wait(barrier, len(peers))

    def piece(ref, slots, a, b):
        rows = pl.ds(pl.multiple_of(c * HALF + b * SUB, 16), SUB)
        cols = pl.ds(pl.multiple_of(a * (Q_ALL // 4), TILE), Q_ALL // 4)
        return ref.at[rows, cols] if slots is None else ref.at[slots, rows, cols]

    for s in (1, 3, 2):
        i = SLOT_OF[4 - s]
        send(piece(weight, None, pa, pb), piece(wbuf, i, pa, pb), y_s.at[s - 1], y_r.at[i], at_y(s))

    def choose(table, s, out):
        first = ((mod(f + s, 4) * 16 + e) * 2 + o) * TILES
        for k in range(TILES):
            out[pl.ds(k * RANK, RANK), :] = table[lax.rem(lang[first + k], LANGS)]

    loads[0].wait()
    for s in (2, 1, 3):
        choose(auv, s, su.at[s - 1])
        send(su.at[s - 1], uu.at[f], u_s.at[s - 1], u_r.at[s - 1], at_y(s))
    choose(auv, 0, uu.at[f])
    loads[2].wait()
    own = ((f * 16 + e) * 2 + o) * TILES
    slot = iota((TILE, Q_ALL), 0)
    for k in range(TILES):
        rows = pl.ds(k * TILE, TILE)
        og[rows, :] = jnp.where(slot < live[own + k], og[rows, :].astype(jnp.float32), 0.0).astype(jnp.bfloat16)

    groups = ((pl.ds(0, 2), (0, 1)), (pl.ds(2, 1), (2,)))

    def b_sends(s, g):
        unit = piece(wbuf, groups[g][0], mod(pa - s, 4), pb)
        send(unit, unit, b_s.at[0, s, g], b_r.at[0, s, g], at_ab(0, 1))
        send(unit, unit, b_s.at[1, s, g], b_r.at[1, s, g], at_ab(0, -1))

    for g in range(2):
        for i in groups[g][1]:
            await_ref(piece(wbuf, i, pa, pb), y_r.at[i])
        unit = piece(wbuf, groups[g][0], pa, pb)
        for s in (2, 1, 3):
            send(unit, unit, a_s.at[s - 1, g], a_r.at[s - 1, g], at_ab(s, 0))
        b_sends(0, g)

    n = iota((T, T), 1)
    chip, y, k = lax.div(n, 64), lax.rem(lax.div(n, 16), 4), lax.rem(lax.div(n, 4), 4)
    source = one_hot(iota((T, T), 0) == ((y * 16 + chip * 2 + c) * 2 + o) * TILES + k)
    langs = jnp.broadcast_to(lang_row[...].astype(jnp.float32), (16, T)).astype(jnp.bfloat16)
    langs = dot(langs, source)[:1]
    m, n = iota((ROWS, T), 0), iota((ROWS, T), 1)
    wanted = (lax.div(m, 4) + o * LANGS).astype(jnp.float32)
    pick[...] = one_hot((langs == wanted) & (lax.rem(n, 4) == lax.rem(m, 4)))

    j, t = iota((ROWS, T), 0), iota((ROWS, T), 1)
    limit = jnp.where(
        t < 2 * TILE,
        jnp.where(t < TILE, live[own], live[own + 1]),
        jnp.where(t < 3 * TILE, live[own + 2], live[own + 3]),
    )
    mask = (lax.div(j, RANK) == lax.div(t, TILE)) & (lax.rem(t, TILE) < limit)
    perm_t = permutation((ROWS, ROWS)).astype(jnp.float32).T.astype(jnp.bfloat16)

    def rows_by_chip(v):
        v = jnp.where(mask, v, 0.0).astype(jnp.bfloat16)
        return dot(perm_t, v).astype(jnp.bfloat16)

    for s in (1, 3, 2):
        await_ref(uu.at[mod(f - s, 4)], u_r.at[s - 1])
    loads[1].wait()
    for s in (2, 1, 3):
        choose(adv, s, sd.at[s - 1])
        send(sd.at[s - 1], dd.at[f], d_s.at[s - 1], d_r.at[s - 1], at_y(s))
    choose(adv, 0, dd.at[f])
    bt = jnp.zeros((ROWS, T), jnp.float32)
    bb = jnp.zeros((T, ROWS), jnp.float32)
    for y in range(YN):
        bt += dot(uu[y], og[:, y * Q_SH : (y + 1) * Q_SH], NT)
        bb += dot(og[:, y * Q_SH : (y + 1) * Q_SH], uu[y], NT)
    tt, jj = iota((T, ROWS), 0), iota((T, ROWS), 1)
    bb = jnp.where(lax.div(jj, RANK) == lax.div(tt, TILE), bb, 0.0).astype(jnp.bfloat16)
    b2[...] = (bb.astype(jnp.float32) * 2.0).astype(jnp.bfloat16)
    btp[...] = rows_by_chip(bt)

    loads[3].wait()
    for s in (2, 1, 3, 0):
        y = mod(f + s, 4)
        part = dot(btp[...], tok[:, pl.ds(pl.multiple_of(y * D_SH, TILE), D_SH)]).astype(jnp.bfloat16)
        if s:
            spd[s - 1] = part
            send(spd.at[s - 1], r1d.at[f], pd_s.at[s - 1], pd_r.at[s - 1], at_y(s))
        else:
            r1d[f] = part

    def spread(r1, r2, s, ssem, rsem):
        y = mod(f - s, 4)

        def one(i, _):
            chip = lax.rem(q + i, CHIPS)
            rcopy(
                r1.at[y, pl.ds(pl.multiple_of(chip * 16, 16), 16)], r2.at[q, y],
                ssem.at[s, i - 1], rsem, at_chip(chip),
            ).start()
            return 0

        lax.fori_loop(1, CHIPS, one, 0)
        pltpu.make_async_copy(r1.at[y, pl.ds(pl.multiple_of(q * 16, 16), 16)], r2.at[q, y], rsem).start()

    def spread_done(r1, r2, ssem):
        def one(i, _):
            rcopy(
                r1.at[0, pl.ds(0, 16)], r2.at[0, 0],
                ssem.at[lax.div(i, CHIPS - 1), lax.rem(i, CHIPS - 1)], ssem.at[0, 0], other,
            ).wait_send()
            return 0

        lax.fori_loop(0, YN * (CHIPS - 1), one, 0)

    spread(r1d, r2d, 0, xd_s, xd_r.at[0])

    for g in range(2):
        for s in (1, 3, 2):
            await_ref(piece(wbuf, groups[g][0], mod(pa - s, 4), pb), a_r.at[s - 1, g])
            b_sends(s, g)

    def block_to_other(rel):
        rows = pl.ds(pl.multiple_of(c * HALF + mod(pb + rel, 4) * SUB, 16), SUB)
        send(wbuf.at[:, rows], wbuf.at[:, rows], c_s.at[rel], c_r.at[rel], other)

    block_to_other(0)

    def pass_on(s, g):
        way = (1 - c) * (2 * lax.rem(z, 2) - 1) + c * (1 if s in (0, 2) else -1)
        unit = piece(wbuf, groups[g][0], mod(pa - s, 4), mod(pb - way, 4))
        await_ref(unit, b_r.at[lax.div(1 - way, 2), s, g])
        send(unit, unit, f_s.at[s, g], f_r.at[s, g], at_ab(0, way))

    def rest(s, g):
        way = (1 - c) * (2 * lax.rem(z, 2) - 1) + c * (1 if s in (0, 2) else -1)
        await_ref(piece(wbuf, groups[g][0], mod(pa - s, 4), mod(pb + way, 4)), b_r.at[lax.div(1 + way, 2), s, g])

    for g in range(2):
        pass_on(0, g)

    def columns(w, y, first, width):
        d = dd[y, :, pl.ds(first, width)]
        value = (dot(og[...], w, NT) + dot(b2[...], d)).astype(jnp.bfloat16)
        igv[:, pl.ds(pl.multiple_of(y * D_SH + first, TILE), width)] = value

    outs = []

    def emit(y, first, width):
        cols = pl.ds(pl.multiple_of(y * D_SH + first, TILE), width)
        cp = pltpu.make_async_copy(igv.at[:, cols], ig.at[:, cols], out_s.at[len(outs)])
        cp.start()
        outs.append(cp)

    loads[4].wait()

    def local_chunk(i, _):
        first = pl.multiple_of(i * LOCAL, TILE)
        columns(wl[pl.ds(first, LOCAL), :], f, first, LOCAL)
        return 0

    lax.fori_loop(0, D_SH // LOCAL, local_chunk, 0)
    emit(f, 0, D_SH)

    for s in (1, 3, 2):
        await_ref(dd.at[mod(f - s, 4)], d_r.at[s - 1])
    ht = jnp.zeros((ROWS, T), jnp.float32)
    for y in range(YN):
        ht += dot(dd[y], tok[:, y * D_SH : (y + 1) * D_SH], NT)
    htp[...] = rows_by_chip(ht)
    for s in (2, 1, 3, 0):
        y = mod(f + s, 4)
        part = dot(htp[...], og[:, pl.ds(pl.multiple_of(y * Q_SH, TILE), Q_SH)]).astype(jnp.bfloat16)
        if s:
            spu[s - 1] = part
            send(spu.at[s - 1], r1u.at[f], pu_s.at[s - 1], pu_r.at[s - 1], at_y(s))
        else:
            r1u[f] = part
    spread(r1u, r2u, 0, xu_s, xu_r.at[0])

    def gathered(i):
        y = mod(f + SLOTS[i], 4)
        for first, width in ((0, 512), (512, 2 * HALF - 512)):
            columns(wbuf[i, first : first + width, :], y, first, width)
        emit(y, 0, 2 * HALF)

    def spread_down(s):
        await_ref(r1d.at[mod(f - s, 4)], pd_r.at[s - 1])
        spread(r1d, r2d, s, xd_s, xd_r.at[0])

    def spread_up(s):
        await_ref(r1u.at[mod(f - s, 4)], pu_r.at[s - 1])
        spread(r1u, r2u, s, xu_s, xu_r.at[0])

    for g in range(2):
        for s in (1, 3, 2):
            pass_on(s, g)
    for g in range(2):
        for s in range(4):
            rest(s, g)
    for rel in (1, 3):
        block_to_other(rel)
    for s in (1, 3, 2):
        spread_down(s)
    for s in (1, 3, 2):
        spread_up(s)

    tail = pl.ds(pl.multiple_of(2 * HALF + c * MINE, 16), MINE)
    for s in (1, 3):
        i = SLOT_OF[4 - s]
        send(weight.at[tail], wbuf.at[i, tail], t_s.at[i], t_r.at[i], at_y(s))

    for g in range(2):
        for s in range(4):
            await_ref(piece(wbuf, groups[g][0], mod(pa - s, 4), mod(pb + 2, 4)), f_r.at[s, g])
    block_to_other(2)
    scale = 2.0 / 256.0
    late = G_ALL - CUT

    def send_sum(width):
        part, there = xout.at[:, pl.ds(0, width)], xin.at[:, pl.ds(0, width)]
        return rcopy(part, there, xc_s.at[0], xc_r.at[0], other)

    def start_gather(width, first):
        mine, place = gv.at[:, pl.ds(0, width)], gg.at[q, :, pl.ds(first, width)]
        for s in (2, 1, 3):
            rcopy(mine, place, g_s.at[s - 1], g_r.at[s - 1], at_chip(chip_of(0, -s))).start()
        rcopy(mine, place, g_s.at[3], g_r.at[3], at_chip(chip_of(1, 0))).start()
        rcopy(mine, place, e_s.at[0], e_r.at[0], other).start()
        pltpu.make_async_copy(mine, place, own_s.at[0]).start()

    await_ref(r2d, xd_r.at[0])
    down = dot(pick[...], r2d[...].reshape(T, D_SH))

    @pl.when(c == 0)
    def _():
        xout[:, : D_SH - CUT] = down[:, CUT:]
        await_ref(xin, xc_r.at[0])
        gv[...] = ((down[:, :CUT] + xin[...]) * scale).astype(jnp.bfloat16)
        start_gather(CUT, 0)

    @pl.when(c == 1)
    def _():
        xout[...] = down[:, :CUT]
        send_sum(CUT).start()

    await_ref(r2u, xu_r.at[0])
    up = dot(pick[...], r2u[...].reshape(T, Q_SH))

    @pl.when(c == 0)
    def _():
        xout[:, D_SH - CUT : late] = up
        send_sum(late).start()

    @pl.when(c == 1)
    def _():
        await_ref(xin.at[:, pl.ds(0, late)], xc_r.at[0])
        gv[:, : D_SH - CUT] = ((down[:, CUT:] + xin[:, : D_SH - CUT]) * scale).astype(jnp.bfloat16)
        gv[:, D_SH - CUT : late] = ((up + xin[:, D_SH - CUT : late]) * scale).astype(jnp.bfloat16)
        start_gather(late, CUT)

    for rel in range(4):
        rows = pl.ds(pl.multiple_of((1 - c) * HALF + mod(pa + rel, 4) * SUB, 16), SUB)
        await_ref(wbuf.at[:, rows], c_r.at[rel])
    gathered(0)

    for i, s in ((1, 1), (0, 3)):
        await_ref(wbuf.at[i, tail], t_r.at[i])
        rows = pl.ds(pl.multiple_of(2 * HALF + c * MINE + (1 - i) * (MINE // 2), 16), MINE // 2)
        send(wbuf.at[i, rows], wbuf.at[2, rows], tf_s.at[i], tf_r.at[i], at_y(s))
    near = wbuf.at[pl.ds(0, 2), tail]
    send(near, near, tc_s.at[0], tc_r.at[0], other)

    def place(dz, s, width, first):
        return gg.at[chip_of(dz, s), :, pl.ds(first, width)]

    def hand_over(width, first, dz, s):
        part = place(dz, s, width, first)
        await_ref(part, g_r.at[s - 1 if dz == 0 else 3 + s])
        rcopy(part, part, e_s.at[dz * 4 + s], e_r.at[dz * 4 + s], other).start()
        return part

    @pl.when(c == 0)
    def _():
        for s in (1, 3, 2):
            part = hand_over(CUT, 0, 0, s)
            rcopy(part, part, g_s.at[3 + s], g_r.at[3 + s], at_chip(chip_of(1, 0))).start()

    @pl.when(c == 1)
    def _():
        part = hand_over(late, CUT, 1, 0)
        for s in (2, 1, 3):
            rcopy(part, part, g_s.at[3 + s], g_r.at[3 + s], at_chip(chip_of(0, -s))).start()

    gathered(1)
    gathered(2)

    theirs = pl.ds(pl.multiple_of(2 * HALF + (1 - c) * MINE, 16), MINE)
    await_ref(wbuf.at[pl.ds(0, 2), theirs], tc_r.at[0])

    def last(i):
        y = mod(f + SLOTS[i], 4)
        columns(wbuf[i, 2 * HALF :, :], y, 2 * HALF, TAIL)
        emit(y, 2 * HALF, TAIL)

    last(0)
    last(1)
    for i in range(2):
        rows = pl.ds(pl.multiple_of(2 * HALF + c * MINE + (1 - i) * (MINE // 2), 16), MINE // 2)
        await_ref(wbuf.at[2, rows], tf_r.at[i])
    far = wbuf.at[2, tail]
    send(far, far, tc_s.at[1], tc_r.at[1], other)

    @pl.when(c == 0)
    def _():
        for s in (0, 1, 3, 2):
            hand_over(CUT, 0, 1, s)

    @pl.when(c == 1)
    def _():
        for dz in (0, 1):
            for s in (1, 3, 2):
                hand_over(late, CUT, dz, s)

    await_ref(wbuf.at[2, theirs], tc_r.at[1])
    last(2)

    def finish(width, first, theirs_width, theirs_first):
        for dz in (0, 1):
            for s in range(4):
                await_ref(place(dz, s, theirs_width, theirs_first), e_r.at[dz * 4 + s])
        mine = gv.at[:, pl.ds(0, width)]
        await_ref(mine, own_s.at[0])
        for i in range(7):
            rcopy(mine, place(0, 0, width, first), g_s.at[i], g_r.at[i], other).wait_send()
        for i in range(8):
            rcopy(mine, place(0, 0, width, first), e_s.at[i], e_r.at[i], other).wait_send()

    @pl.when(c == 0)
    def _():
        send_sum(late).wait_send()
        finish(CUT, 0, late, CUT)

    @pl.when(c == 1)
    def _():
        send_sum(CUT).wait_send()
        finish(late, CUT, CUT, 0)

    for cp in sends:
        cp.wait_send()
    spread_done(r1d, r2d, xd_s)
    spread_done(r1u, r2u, xu_s)
    for cp in outs:
        cp.wait()


def finish_kernel(gg, ig_in, down, up, ig, buf, dv, uv, iv, in_s, out_s):
    loads, through = [], []
    for g in range(4):
        part, rows = pl.ds(g * 32, 32), pl.ds(g * TILE, TILE)
        loads.append(pltpu.make_async_copy(gg.at[:, part], buf.at[:, part], in_s.at[0, g]))
        through.append(pltpu.make_async_copy(ig_in.at[rows], iv.at[rows], in_s.at[1, g]))
        loads[-1].start()
        through[-1].start()
    perm = permutation((ROWS, ROWS))
    outs = []
    for g in range(4):
        loads[g].wait()
        for h in (2 * g, 2 * g + 1):
            rows = buf[:, h * 16 : (h + 1) * 16, :].reshape(ROWS, G_ALL)
            rows = dot(perm, rows).astype(jnp.bfloat16).reshape(4, RANK, G_ALL)
            dv[h * 4 : (h + 1) * 4] = rows[:, :, :D_SH]
            uv[h * 4 : (h + 1) * 4] = rows[:, :, D_SH:]
        for i, (src, dst) in enumerate(((dv, down), (uv, up))):
            cp = pltpu.make_async_copy(src.at[g * 8 : (g + 1) * 8], dst.at[g * 8 : (g + 1) * 8], out_s.at[i, g])
            cp.start()
            outs.append(cp)
        through[g].wait()
        rows = pl.ds(g * TILE, TILE)
        cp = pltpu.make_async_copy(iv.at[rows], ig.at[rows], out_s.at[2, g])
        cp.start()
        outs.append(cp)
    for cp in outs:
        cp.wait()


def on_device(tokens, output_gradient, tile_language, tile_live_count, frozen_weight, adapter_down, adapter_up):
    bf = jnp.bfloat16
    hbm, smem, vmem = (pl.BlockSpec(memory_space=s) for s in (pl.ANY, pltpu.SMEM, pltpu.VMEM))
    sem = pltpu.SemaphoreType.DMA

    def sems(*shapes):
        return [sem(s) for s in shapes]

    def buf(*shape, dtype=bf):
        return pltpu.VMEM(shape, dtype)

    ig, gg = pl.pallas_call(
        main_kernel,
        out_shape=(
            jax.ShapeDtypeStruct((T, D_ALL), bf),
            jax.ShapeDtypeStruct((CHIPS, ROWS, G_ALL), bf),
        ),
        in_specs=[smem, smem, vmem, hbm, hbm, hbm, hbm, hbm],
        out_specs=(hbm, hbm),
        scratch_shapes=[
            buf(3, D_SH, Q_ALL),
            buf(D_SH, Q_ALL),
            buf(T, D_ALL),
            buf(T, Q_ALL),
            buf(LANGS, RANK, D_SH),
            buf(LANGS, RANK, Q_SH),
            buf(3, ROWS, Q_SH),
            buf(3, ROWS, D_SH),
            buf(YN, ROWS, Q_SH),
            buf(YN, ROWS, D_SH),
            buf(3, ROWS, D_SH),
            buf(3, ROWS, Q_SH),
            buf(YN, ROWS, D_SH),
            buf(YN, ROWS, Q_SH),
            buf(CHIPS, YN, 16, D_SH),
            buf(CHIPS, YN, 16, Q_SH),
            buf(ROWS, CUT, dtype=jnp.float32),
            buf(ROWS, CUT, dtype=jnp.float32),
            buf(ROWS, CUT),
            buf(T, D_ALL),
            buf(T, ROWS),
            buf(ROWS, T),
            buf(ROWS, T),
            buf(ROWS, T),
            *sems((5,), (3,), (3,), (3, 2), (3, 2), (2, 4, 2), (2, 4, 2), (4, 2), (4, 2), (4,), (4,)),
            *sems((2,), (2,), (2,), (2,), (2,), (2,)),
            *sems((3,), (3,), (3,), (3,), (3,), (3,), (3,), (3,), (4, 7), (1,), (4, 7), (1,)),
            *sems((1,), (1,), (7,), (7,), (8,), (8,), (1,), (7,)),
        ],
        compiler_params=pltpu.CompilerParams(
            collective_id=0, has_side_effects=True, vmem_limit_bytes=58 * 2**20
        ),
        cost_estimate=pl.CostEstimate(flops=12 * 10**9, bytes_accessed=40 * 10**6, transcendentals=0),
        name="exchange",
    )(
        tile_language, tile_live_count, tile_language.reshape(1, T),
        tokens, output_gradient, frozen_weight, adapter_down, adapter_up,
    )
    down, up, ig = pl.pallas_call(
        finish_kernel,
        out_shape=(
            jax.ShapeDtypeStruct((LANGS, RANK, D_SH), bf),
            jax.ShapeDtypeStruct((LANGS, RANK, Q_SH), bf),
            jax.ShapeDtypeStruct((T, D_ALL), bf),
        ),
        in_specs=[hbm, hbm],
        out_specs=(hbm, hbm, hbm),
        scratch_shapes=[
            buf(CHIPS, ROWS, G_ALL), buf(LANGS, RANK, D_SH), buf(LANGS, RANK, Q_SH), buf(T, D_ALL),
            *sems((2, 4), (3, 4)),
        ],
        compiler_params=pltpu.CompilerParams(vmem_limit_bytes=60 * 2**20),
        name="finish",
    )(gg, ig)
    return ig, down, up


def solution(mesh):
    tok = P(("fsdp", "dp", "owner"), None)
    adapter = P("owner", None, "fsdp")
    return jax.shard_map(
        on_device,
        mesh=mesh,
        in_specs=(tok, tok, P(), P(), P("fsdp", None), adapter, adapter),
        out_specs=(tok, adapter, adapter),
        check_vma=False,
    )
```

```python
import functools

import jax
import jax.numpy as jnp
from jax import lax
from jax.experimental import pallas as pl
from jax.experimental.pallas import tpu as pltpu
from jax.sharding import PartitionSpec as P

MESH = pl.DeviceIdType.MESH
NT = (((1,), (1,)), ((), ()))
NN = (((1,), (0,)), ((), ()))

TILE = 128
TILES = 4
RANK = 32
ROWS = TILES * RANK
LANGS = 32
YN = 4
CHIPS = 8
T = TILE * TILES
D_ALL, Q_ALL = 4608, 2048
D_SH, Q_SH = D_ALL // YN, Q_ALL // YN
G_ALL = D_SH + Q_SH
SUB = 112
HALF = 4 * SUB
TAIL = D_SH - 2 * HALF
MINE = TAIL // 2
LOCAL = 384
SLOTS = (1, 3, 2)
SLOT_OF = {1: 0, 3: 1, 2: 2}
PARTS = ((0, 640), (640, 512), (D_SH, Q_SH))


def dot(a, b, dims=NN):
    return lax.dot_general(a, b, dims, preferred_element_type=jnp.float32)


def one_hot(cond):
    return cond.astype(jnp.float32).astype(jnp.bfloat16)


def iota(shape, dim):
    return lax.broadcasted_iota(jnp.int32, shape, dim)


def permutation(shape):
    i, j = iota(shape, 0), iota(shape, 1)
    k, q, r = lax.div(lax.rem(j, 16), 4), lax.div(j, 16), lax.rem(j, 4)
    return one_hot(i == k * RANK + q * 4 + r)


def main_kernel(
    lang, live, lang_row, tokens, grad, weight, adown, aup,
    ig, gg,
    wbuf, wl, tok, og, adv, auv, su, sd, uu, dd, spd, spu, r1d, r1u, r2d, r2u, xout, xin, gv, b2, btp, htp, pick,
    in_sem, y_s, y_r, a_s, a_r, b_s, b_r, f_s, f_r, c_s, c_r, t_s, t_r, tf_s, tf_r, tc_s, tc_r,
    u_s, u_r, d_s, d_r, pd_s, pd_r, pu_s, pu_r, xd_s, xd_r, xu_s, xu_r, xc_s, xc_r, g_s, g_r, e_s, e_r, own_s,
):
    f, e, o = lax.axis_index("fsdp"), lax.axis_index("dp"), lax.axis_index("owner")
    q, c = lax.div(e, 2), lax.rem(e, 2)
    x, zl = lax.rem(q, 4), lax.div(q, 4)
    z = o * 2 + zl
    pa = x * (1 - c) + z * c
    pb = z * (1 - c) + x * c

    def mod(v, n):
        return lax.rem(v + n, n)

    def at_ab(da, db):
        a, b = mod(pa + da, 4), mod(pb + db, 4)
        xx, zz = a * (1 - c) + b * c, b * (1 - c) + a * c
        return (f, lax.rem(zz, 2) * 8 + xx * 2 + c, lax.div(zz, 2))

    def at_y(s):
        return (mod(f + s, 4), e, o)

    def at_chip(chip):
        return (f, chip * 2 + c, o)

    def chip_of(dz, s):
        return lax.rem(zl + dz, 2) * 4 + mod(x - s, 4)

    other = (f, q * 2 + 1 - c, o)

    def rcopy(src, dst, ssem, rsem, dev):
        return pltpu.make_async_remote_copy(
            src_ref=src, dst_ref=dst, send_sem=ssem, recv_sem=rsem, device_id=dev, device_id_type=MESH
        )

    def await_ref(ref, sem):
        pltpu.make_async_copy(ref, ref, sem).wait()

    sends = []

    def send(*args):
        cp = rcopy(*args)
        cp.start()
        sends.append(cp)

    loads = [
        pltpu.make_async_copy(s, d, in_sem.at[i])
        for i, (s, d) in enumerate(((aup, auv), (adown, adv), (grad, og), (tokens, tok), (weight, wl)))
    ]
    for cp in loads:
        cp.start()

    barrier = pltpu.get_barrier_semaphore()
    peers = [at_y(s) for s in (1, 2, 3)]
    peers += [at_ab(s, 0) for s in (1, 2, 3)] + [at_ab(0, 1), at_ab(0, -1)]
    peers += [at_chip(lax.rem(q + s, CHIPS)) for s in range(1, CHIPS)] + [other]
    for dev in peers:
        pl.semaphore_signal(barrier, inc=1, device_id=dev, device_id_type=MESH)
    pl.semaphore_wait(barrier, len(peers))

    def piece(ref, slots, a, b):
        rows = pl.ds(pl.multiple_of(c * HALF + b * SUB, 16), SUB)
        cols = pl.ds(pl.multiple_of(a * (Q_ALL // 4), TILE), Q_ALL // 4)
        return ref.at[rows, cols] if slots is None else ref.at[slots, rows, cols]

    for s in (1, 3, 2):
        i = SLOT_OF[4 - s]
        send(piece(weight, None, pa, pb), piece(wbuf, i, pa, pb), y_s.at[s - 1], y_r.at[i], at_y(s))

    def choose(table, s, out):
        first = ((mod(f + s, 4) * 16 + e) * 2 + o) * TILES
        for k in range(TILES):
            out[pl.ds(k * RANK, RANK), :] = table[lax.rem(lang[first + k], LANGS)]

    loads[2].wait()
    own = ((f * 16 + e) * 2 + o) * TILES
    slot = iota((TILE, Q_ALL), 0)
    for k in range(TILES):
        rows = pl.ds(k * TILE, TILE)
        og[rows, :] = jnp.where(slot < live[own + k], og[rows, :].astype(jnp.float32), 0.0).astype(jnp.bfloat16)

    groups = ((pl.ds(0, 2), (0, 1)), (pl.ds(2, 1), (2,)))

    def b_sends(s, g):
        unit = piece(wbuf, groups[g][0], mod(pa - s, 4), pb)
        send(unit, unit, b_s.at[0, s, g], b_r.at[0, s, g], at_ab(0, 1))
        send(unit, unit, b_s.at[1, s, g], b_r.at[1, s, g], at_ab(0, -1))

    for g in range(2):
        for i in groups[g][1]:
            await_ref(piece(wbuf, i, pa, pb), y_r.at[i])
        unit = piece(wbuf, groups[g][0], pa, pb)
        for s in (2, 1, 3):
            send(unit, unit, a_s.at[s - 1, g], a_r.at[s - 1, g], at_ab(s, 0))
        if g == 0:
            loads[0].wait()
            for s in (2, 1, 3):
                choose(auv, s, su.at[s - 1])
                send(su.at[s - 1], uu.at[f], u_s.at[s - 1], u_r.at[s - 1], at_y(s))

    choose(auv, 0, uu.at[f])
    n = iota((T, T), 1)
    chip, y, k = lax.div(n, 64), lax.rem(lax.div(n, 16), 4), lax.rem(lax.div(n, 4), 4)
    source = one_hot(iota((T, T), 0) == ((y * 16 + chip * 2 + c) * 2 + o) * TILES + k)
    langs = jnp.broadcast_to(lang_row[...].astype(jnp.float32), (16, T)).astype(jnp.bfloat16)
    langs = dot(langs, source)[:1]
    m, n = iota((ROWS, T), 0), iota((ROWS, T), 1)
    wanted = (lax.div(m, 4) + o * LANGS).astype(jnp.float32)
    pick[...] = one_hot((langs == wanted) & (lax.rem(n, 4) == lax.rem(m, 4)))

    j, t = iota((ROWS, T), 0), iota((ROWS, T), 1)
    limit = jnp.where(
        t < 2 * TILE,
        jnp.where(t < TILE, live[own], live[own + 1]),
        jnp.where(t < 3 * TILE, live[own + 2], live[own + 3]),
    )
    mask = (lax.div(j, RANK) == lax.div(t, TILE)) & (lax.rem(t, TILE) < limit)
    perm_t = permutation((ROWS, ROWS)).astype(jnp.float32).T.astype(jnp.bfloat16)

    def rows_by_chip(v):
        v = jnp.where(mask, v, 0.0).astype(jnp.bfloat16)
        return dot(perm_t, v).astype(jnp.bfloat16)

    for s in (1, 3, 2):
        await_ref(uu.at[mod(f - s, 4)], u_r.at[s - 1])
    for g in range(2):
        b_sends(0, g)
    bt = jnp.zeros((ROWS, T), jnp.float32)
    bb = jnp.zeros((T, ROWS), jnp.float32)
    for y in range(YN):
        bt += dot(uu[y], og[:, y * Q_SH : (y + 1) * Q_SH], NT)
        bb += dot(og[:, y * Q_SH : (y + 1) * Q_SH], uu[y], NT)
    tt, jj = iota((T, ROWS), 0), iota((T, ROWS), 1)
    bb = jnp.where(lax.div(jj, RANK) == lax.div(tt, TILE), bb, 0.0).astype(jnp.bfloat16)
    b2[...] = (bb.astype(jnp.float32) * 2.0).astype(jnp.bfloat16)
    btp[...] = rows_by_chip(bt)

    loads[3].wait()
    for s in (2, 1, 3, 0):
        y = mod(f + s, 4)
        part = dot(btp[...], tok[:, pl.ds(pl.multiple_of(y * D_SH, TILE), D_SH)]).astype(jnp.bfloat16)
        if s:
            spd[s - 1] = part
            send(spd.at[s - 1], r1d.at[f], pd_s.at[s - 1], pd_r.at[s - 1], at_y(s))
        else:
            r1d[f] = part

    loads[1].wait()
    for s in (2, 1, 3):
        choose(adv, s, sd.at[s - 1])
        send(sd.at[s - 1], dd.at[f], d_s.at[s - 1], d_r.at[s - 1], at_y(s))
    choose(adv, 0, dd.at[f])

    def spread(r1, r2, s, ssem, rsem):
        y = mod(f - s, 4)

        def one(i, _):
            chip = lax.rem(q + i, CHIPS)
            rcopy(
                r1.at[y, pl.ds(pl.multiple_of(chip * 16, 16), 16)], r2.at[q, y],
                ssem.at[s, i - 1], rsem, at_chip(chip),
            ).start()
            return 0

        lax.fori_loop(1, CHIPS, one, 0)
        pltpu.make_async_copy(r1.at[y, pl.ds(pl.multiple_of(q * 16, 16), 16)], r2.at[q, y], rsem).start()

    def spread_done(r1, r2, ssem):
        def one(i, _):
            rcopy(
                r1.at[0, pl.ds(0, 16)], r2.at[0, 0],
                ssem.at[lax.div(i, CHIPS - 1), lax.rem(i, CHIPS - 1)], ssem.at[0, 0], other,
            ).wait_send()
            return 0

        lax.fori_loop(0, YN * (CHIPS - 1), one, 0)

    spread(r1d, r2d, 0, xd_s, xd_r.at[0])

    for g in range(2):
        for s in (1, 3, 2):
            await_ref(piece(wbuf, groups[g][0], mod(pa - s, 4), pb), a_r.at[s - 1, g])
            b_sends(s, g)

    def block_to_other(rel):
        rows = pl.ds(pl.multiple_of(c * HALF + mod(pb + rel, 4) * SUB, 16), SUB)
        send(wbuf.at[:, rows], wbuf.at[:, rows], c_s.at[rel], c_r.at[rel], other)

    block_to_other(0)

    def pass_on(s, g):
        way = (1 - c) * (2 * lax.rem(z, 2) - 1) + c * (1 if s in (0, 2) else -1)
        unit = piece(wbuf, groups[g][0], mod(pa - s, 4), mod(pb - way, 4))
        await_ref(unit, b_r.at[lax.div(1 - way, 2), s, g])
        send(unit, unit, f_s.at[s, g], f_r.at[s, g], at_ab(0, way))

    def rest(s, g):
        way = (1 - c) * (2 * lax.rem(z, 2) - 1) + c * (1 if s in (0, 2) else -1)
        await_ref(piece(wbuf, groups[g][0], mod(pa - s, 4), mod(pb + way, 4)), b_r.at[lax.div(1 + way, 2), s, g])

    for g in range(2):
        pass_on(0, g)

    def columns(w, y, first, width):
        d = dd[y, :, pl.ds(first, width)]
        value = (dot(og[...], w, NT) + dot(b2[...], d)).astype(jnp.bfloat16)
        ig[:, pl.ds(pl.multiple_of(y * D_SH + first, TILE), width)] = value

    loads[4].wait()

    def local_chunk(i, _):
        first = pl.multiple_of(i * LOCAL, TILE)
        columns(wl[pl.ds(first, LOCAL), :], f, first, LOCAL)
        return 0

    lax.fori_loop(0, D_SH // LOCAL, local_chunk, 0)

    def gathered(i):
        y = mod(f + SLOTS[i], 4)
        for first, width in ((0, 512), (512, 2 * HALF - 512)):
            columns(wbuf[i, first : first + width, :], y, first, width)

    def spread_down(s):
        await_ref(r1d.at[mod(f - s, 4)], pd_r.at[s - 1])
        spread(r1d, r2d, s, xd_s, xd_r.at[0])

    def spread_up(s):
        await_ref(r1u.at[mod(f - s, 4)], pu_r.at[s - 1])
        spread(r1u, r2u, s, xu_s, xu_r.at[0])

    for s in (1, 3, 2):
        spread_down(s)
    for g in range(2):
        for s in (1, 3, 2):
            pass_on(s, g)
    for g in range(2):
        for s in range(4):
            rest(s, g)
    for rel in (1, 3):
        block_to_other(rel)
    for s in (1, 3, 2):
        await_ref(dd.at[mod(f - s, 4)], d_r.at[s - 1])
    ht = jnp.zeros((ROWS, T), jnp.float32)
    for y in range(YN):
        ht += dot(dd[y], tok[:, y * D_SH : (y + 1) * D_SH], NT)
    htp[...] = rows_by_chip(ht)
    for s in (2, 1, 3, 0):
        y = mod(f + s, 4)
        part = dot(htp[...], og[:, pl.ds(pl.multiple_of(y * Q_SH, TILE), Q_SH)]).astype(jnp.bfloat16)
        if s:
            spu[s - 1] = part
            send(spu.at[s - 1], r1u.at[f], pu_s.at[s - 1], pu_r.at[s - 1], at_y(s))
        else:
            r1u[f] = part
    spread(r1u, r2u, 0, xu_s, xu_r.at[0])

    tail = pl.ds(pl.multiple_of(2 * HALF + c * MINE, 16), MINE)
    for s in (1, 3):
        i = SLOT_OF[4 - s]
        send(weight.at[tail], wbuf.at[i, tail], t_s.at[i], t_r.at[i], at_y(s))

    for g in range(2):
        for s in range(4):
            await_ref(piece(wbuf, groups[g][0], mod(pa - s, 4), mod(pb + 2, 4)), f_r.at[s, g])
    block_to_other(2)

    scale = 2.0 / 256.0

    def send_sum(width):
        part, there = xout.at[:, pl.ds(0, width)], xin.at[:, pl.ds(0, width)]
        return rcopy(part, there, xc_s.at[0], xc_r.at[0], other)

    def place(dz, s, r):
        return gg.at[chip_of(dz, s), :, pl.ds(*PARTS[r])]

    def mine(r):
        return gv.at[:, pl.ds(PARTS[r][0] % D_SH, PARTS[r][1])]

    def to_x(src, dst, r, k):
        for s in (2, 1, 3):
            rcopy(src, dst, g_s.at[r % 2, k + s - 1], g_r.at[r % 2, k + s - 1], at_chip(chip_of(0, -s))).start()

    def to_z(src, dst, r, k):
        rcopy(src, dst, g_s.at[r % 2, k], g_r.at[r % 2, k], at_chip(chip_of(1, 0))).start()

    def to_core(src, dst, r, k):
        rcopy(src, dst, e_s.at[r % 2, k], e_r.at[r % 2, k], other).start()

    def hand_over(dz, s, r):
        part = place(dz, s, r)
        await_ref(part, g_r.at[r % 2, s - 1 if dz == 0 else 3 + s])
        to_core(part, part, r, dz * 4 + s)
        return part

    await_ref(r2d, xd_r.at[0])
    down = dot(pick[...], r2d[...].reshape(T, D_SH))

    @pl.when(c == 1)
    def _():
        xout[...] = down
        send_sum(D_SH).start()

    for s in (1, 3, 2):
        spread_up(s)

    @pl.when(c == 0)
    def _():
        await_ref(xin, xc_r.at[0])
        gv[...] = ((down + xin[...]) * scale).astype(jnp.bfloat16)
        to_z(mine(1), place(0, 0, 1), 1, 3)
        to_x(mine(0), place(0, 0, 0), 0, 0)
        to_x(mine(1), place(0, 0, 1), 1, 0)
        to_z(mine(0), place(0, 0, 0), 0, 3)
        for r in (0, 1):
            to_core(mine(r), place(0, 0, r), r, 0)
            pltpu.make_async_copy(mine(r), place(0, 0, r), own_s.at[r]).start()

    for rel in range(4):
        rows = pl.ds(pl.multiple_of((1 - c) * HALF + mod(pa + rel, 4) * SUB, 16), SUB)
        await_ref(wbuf.at[:, rows], c_r.at[rel])
    gathered(0)

    await_ref(r2u, xu_r.at[0])
    up = dot(pick[...], r2u[...].reshape(T, Q_SH))

    @pl.when(c == 0)
    def _():
        xout[:, :Q_SH] = up
        send_sum(Q_SH).start()
        part = hand_over(1, 0, 1)
        to_x(part, part, 1, 4)
        for s in (1, 3, 2):
            part = hand_over(0, s, 0)
            to_z(part, part, 0, 3 + s)

    @pl.when(c == 1)
    def _():
        await_ref(xin.at[:, pl.ds(0, Q_SH)], xc_r.at[0])
        gv[:, :Q_SH] = ((up + xin[:, :Q_SH]) * scale).astype(jnp.bfloat16)
        to_z(mine(2), place(0, 0, 2), 2, 3)
        to_x(mine(2), place(0, 0, 2), 2, 0)
        to_core(mine(2), place(0, 0, 2), 2, 0)
        pltpu.make_async_copy(mine(2), place(0, 0, 2), own_s.at[0]).start()

    for i, s in ((1, 1), (0, 3)):
        await_ref(wbuf.at[i, tail], t_r.at[i])
        rows = pl.ds(pl.multiple_of(2 * HALF + c * MINE + (1 - i) * (MINE // 2), 16), MINE // 2)
        send(wbuf.at[i, rows], wbuf.at[2, rows], tf_s.at[i], tf_r.at[i], at_y(s))
    near = wbuf.at[pl.ds(0, 2), tail]
    send(near, near, tc_s.at[0], tc_r.at[0], other)

    @pl.when(c == 1)
    def _():
        part = hand_over(1, 0, 2)
        to_x(part, part, 2, 4)

    gathered(1)
    gathered(2)
    theirs = pl.ds(pl.multiple_of(2 * HALF + (1 - c) * MINE, 16), MINE)
    await_ref(wbuf.at[pl.ds(0, 2), theirs], tc_r.at[0])

    w = wbuf[0:2, 2 * HALF :, :].reshape(2 * TAIL, Q_ALL)
    near_sum = dot(og[...], w, NT)
    for i in range(2):
        y = mod(f + SLOTS[i], 4)
        value = near_sum[:, i * TAIL : (i + 1) * TAIL] + dot(b2[...], dd[y, :, 2 * HALF :])
        ig[:, pl.ds(pl.multiple_of(y * D_SH + 2 * HALF, TILE), TAIL)] = value.astype(jnp.bfloat16)
    for i in range(2):
        rows = pl.ds(pl.multiple_of(2 * HALF + c * MINE + (1 - i) * (MINE // 2), 16), MINE // 2)
        await_ref(wbuf.at[2, rows], tf_r.at[i])
    far = wbuf.at[2, tail]
    send(far, far, tc_s.at[1], tc_r.at[1], other)

    @pl.when(c == 0)
    def _():
        for dz in (0, 1):
            for s in (1, 3, 2):
                hand_over(dz, s, 1)
        for s in (0, 1, 3, 2):
            hand_over(1, s, 0)

    @pl.when(c == 1)
    def _():
        for dz in (0, 1):
            for s in (1, 3, 2):
                hand_over(dz, s, 2)

    await_ref(wbuf.at[2, theirs], tc_r.at[1])
    columns(wbuf[2, 2 * HALF :, :], mod(f + SLOTS[2], 4), 2 * HALF, TAIL)

    def finish(ours, theirs, width):
        for r in theirs:
            for dz in (0, 1):
                for s in range(4):
                    await_ref(place(dz, s, r), e_r.at[r % 2, dz * 4 + s])
        send_sum(width).wait_send()
        for r in ours:
            await_ref(mine(r), own_s.at[r % 2])
            for k in range(7):
                rcopy(mine(r), place(0, 0, r), g_s.at[r % 2, k], g_r.at[r % 2, k], other).wait_send()
            for k in range(8):
                rcopy(mine(r), place(0, 0, r), e_s.at[r % 2, k], e_r.at[r % 2, k], other).wait_send()

    @pl.when(c == 0)
    def _():
        finish((0, 1), (2,), Q_SH)

    @pl.when(c == 1)
    def _():
        finish((2,), (0, 1), D_SH)

    for cp in sends:
        cp.wait_send()
    spread_done(r1d, r2d, xd_s)
    spread_done(r1u, r2u, xu_s)


def finish_kernel(gg, ig_in, down, up, ig, dv, uv, out_s):
    outs = []

    def emit(src, dst, i, g):
        cp = pltpu.make_async_copy(src, dst, out_s.at[i, g])
        cp.start()
        outs.append(cp)

    for g in range(4):
        rows = pl.ds(g * TILE, TILE)
        emit(ig_in.at[rows], ig.at[rows], 2, g)
    perm = permutation((ROWS, ROWS))
    for g in range(4):
        for h in (2 * g, 2 * g + 1):
            rows = gg[:, h * 16 : (h + 1) * 16, :].reshape(ROWS, G_ALL)
            rows = dot(perm, rows).astype(jnp.bfloat16).reshape(4, RANK, G_ALL)
            dv[h * 4 : (h + 1) * 4] = rows[:, :, :D_SH]
            uv[h * 4 : (h + 1) * 4] = rows[:, :, D_SH:]
        part = pl.ds(g * 8, 8)
        emit(dv.at[part], down.at[part], 0, g)
        emit(uv.at[part], up.at[part], 1, g)
    for cp in outs:
        cp.wait()


def on_device(tokens, output_gradient, tile_language, tile_live_count, frozen_weight, adapter_down, adapter_up):
    bf = jnp.bfloat16
    pin = pltpu.with_memory_space_constraint
    tokens, output_gradient, frozen_weight, adapter_down, adapter_up = (
        pin(a, pltpu.HBM) for a in (tokens, output_gradient, frozen_weight, adapter_down, adapter_up)
    )
    hbm, smem, vmem = (pl.BlockSpec(memory_space=s) for s in (pl.ANY, pltpu.SMEM, pltpu.VMEM))
    sem = pltpu.SemaphoreType.DMA

    def sems(*shapes):
        return [sem(s) for s in shapes]

    def buf(*shape, dtype=bf):
        return pltpu.VMEM(shape, dtype)

    ig, gg = pl.pallas_call(
        main_kernel,
        out_shape=(
            buf(T, D_ALL),
            buf(CHIPS, ROWS, G_ALL),
        ),
        in_specs=[smem, smem, vmem, hbm, hbm, hbm, hbm, hbm],
        out_specs=(vmem, vmem),
        scratch_shapes=[
            buf(3, D_SH, Q_ALL),
            buf(D_SH, Q_ALL),
            buf(T, D_ALL),
            buf(T, Q_ALL),
            buf(LANGS, RANK, D_SH),
            buf(LANGS, RANK, Q_SH),
            buf(3, ROWS, Q_SH),
            buf(3, ROWS, D_SH),
            buf(YN, ROWS, Q_SH),
            buf(YN, ROWS, D_SH),
            buf(3, ROWS, D_SH),
            buf(3, ROWS, Q_SH),
            buf(YN, ROWS, D_SH),
            buf(YN, ROWS, Q_SH),
            buf(CHIPS, YN, 16, D_SH),
            buf(CHIPS, YN, 16, Q_SH),
            buf(ROWS, D_SH, dtype=jnp.float32),
            buf(ROWS, D_SH, dtype=jnp.float32),
            buf(ROWS, D_SH),
            buf(T, ROWS),
            buf(ROWS, T),
            buf(ROWS, T),
            buf(ROWS, T),
            *sems((5,), (3,), (3,), (3, 2), (3, 2), (2, 4, 2), (2, 4, 2), (4, 2), (4, 2), (4,), (4,)),
            *sems((2,), (2,), (2,), (2,), (2,), (2,)),
            *sems((3,), (3,), (3,), (3,), (3,), (3,), (3,), (3,), (4, 7), (1,), (4, 7), (1,)),
            *sems((1,), (1,), (2, 7), (2, 7), (2, 8), (2, 8), (2,)),
        ],
        compiler_params=pltpu.CompilerParams(
            collective_id=0, has_side_effects=True, vmem_limit_bytes=46 * 2**20
        ),
        cost_estimate=pl.CostEstimate(flops=12 * 10**9, bytes_accessed=40 * 10**6, transcendentals=0),
        name="exchange",
    )(
        pin(tile_language, pltpu.HBM), pin(tile_live_count, pltpu.HBM), tile_language.reshape(1, T),
        tokens, output_gradient, frozen_weight, adapter_down, adapter_up,
    )
    down, up, ig = pl.pallas_call(
        finish_kernel,
        out_shape=(
            jax.ShapeDtypeStruct((LANGS, RANK, D_SH), bf),
            jax.ShapeDtypeStruct((LANGS, RANK, Q_SH), bf),
            jax.ShapeDtypeStruct((T, D_ALL), bf),
        ),
        in_specs=[vmem, vmem],
        out_specs=(hbm, hbm, hbm),
        scratch_shapes=[buf(LANGS, RANK, D_SH), buf(LANGS, RANK, Q_SH), sem((3, 4))],
        compiler_params=pltpu.CompilerParams(vmem_limit_bytes=16 * 2**20),
        name="finish",
    )(pin(gg, pltpu.VMEM), pin(ig, pltpu.VMEM))
    return ig, down, up


def solution(mesh):
    tok = P(("fsdp", "dp", "owner"), None)
    adapter = P("owner", None, "fsdp")
    return jax.shard_map(
        on_device,
        mesh=mesh,
        in_specs=(tok, tok, P(), P(), P("fsdp", None), adapter, adapter),
        out_specs=(tok, adapter, adapter),
        check_vma=False,
    )
```

```python
import functools

import jax
import jax.numpy as jnp
from jax import lax
from jax.experimental import pallas as pl
from jax.experimental.pallas import tpu as pltpu
from jax.sharding import PartitionSpec as P

MESH = pl.DeviceIdType.MESH
NT = (((1,), (1,)), ((), ()))
NN = (((1,), (0,)), ((), ()))

TILE = 128
TILES = 4
RANK = 32
ROWS = TILES * RANK
LANGS = 32
YN = 4
CHIPS = 8
T = TILE * TILES
D_ALL, Q_ALL = 4608, 2048
D_SH, Q_SH = D_ALL // YN, Q_ALL // YN
G_ALL = D_SH + Q_SH
SUBS = (96, 16)
MAIN = 4 * SUBS[0]
HALF = 4 * sum(SUBS)
TAIL = D_SH - 2 * HALF
MINE = TAIL // 2
LOCAL = 384
SLOTS = (1, 3, 2)
SLOT_OF = {1: 0, 3: 1, 2: 2}
PARTS = ((0, 768), (768, 384), (D_SH, 256), (D_SH + 256, 256))


def dot(a, b, dims=NN):
    return lax.dot_general(a, b, dims, preferred_element_type=jnp.float32)


def one_hot(cond):
    return cond.astype(jnp.float32).astype(jnp.bfloat16)


def iota(shape, dim):
    return lax.broadcasted_iota(jnp.int32, shape, dim)


def permutation(shape):
    i, j = iota(shape, 0), iota(shape, 1)
    k, q, r = lax.div(lax.rem(j, 16), 4), lax.div(j, 16), lax.rem(j, 4)
    return one_hot(i == k * RANK + q * 4 + r)


def main_kernel(
    lang, live, lang_row, tokens, grad, weight, adown, aup,
    ig, gg,
    wbuf, wl, tok, og, adv, auv, su, sd, uu, dd, spd, spu, r1d, r1u, r2d, r2u, xout, xin, gv, b2, btp, htp, pick,
    in_sem, w_s, y_r, a_r, b_r, f_r, c_r, t_r, tf_r, tc_r,
    u_s, u_r, d_s, d_r, pd_s, pd_r, pu_s, pu_r, xd_s, xd_r, xu_s, xu_r, xc_s, xc_r, g_s, g_r, e_s, e_r, own_s,
):
    f, e, o = lax.axis_index("fsdp"), lax.axis_index("dp"), lax.axis_index("owner")
    q, c = lax.div(e, 2), lax.rem(e, 2)
    x, zl = lax.rem(q, 4), lax.div(q, 4)
    z = o * 2 + zl
    pa = (x * (1 - c) + z * c, x)
    pb = (z * (1 - c) + x * c, z)
    swap = (c, 0)

    def mod(v, n):
        return lax.rem(v + n, n)

    def at_ab(t, da, db):
        a, b = mod(pa[t] + da, 4), mod(pb[t] + db, 4)
        xx, zz = a * (1 - swap[t]) + b * swap[t], b * (1 - swap[t]) + a * swap[t]
        return (f, lax.rem(zz, 2) * 8 + xx * 2 + c, lax.div(zz, 2))

    def at_y(s):
        return (mod(f + s, 4), e, o)

    def at_chip(chip):
        return (f, chip * 2 + c, o)

    def chip_of(dz, s):
        return lax.rem(zl + dz, 2) * 4 + mod(x - s, 4)

    other = (f, q * 2 + 1 - c, o)

    def rcopy(src, dst, ssem, rsem, dev):
        return pltpu.make_async_remote_copy(
            src_ref=src, dst_ref=dst, send_sem=ssem, recv_sem=rsem, device_id=dev, device_id_type=MESH
        )

    def await_ref(ref, sem):
        pltpu.make_async_copy(ref, ref, sem).wait()

    def send(*args):
        rcopy(*args).start()

    loads = [
        pltpu.make_async_copy(s, d, in_sem.at[i])
        for i, (s, d) in enumerate(((aup, auv), (adown, adv), (grad, og), (tokens, tok), (weight, wl)))
    ]
    for cp in loads:
        cp.start()

    barrier = pltpu.get_barrier_semaphore()
    peers = [at_y(s) for s in (1, 2, 3)]
    for t in range(2):
        peers += [at_ab(t, s, 0) for s in (1, 2, 3)] + [at_ab(t, 0, 1), at_ab(t, 0, -1)]
    peers += [at_chip(lax.rem(q + s, CHIPS)) for s in range(1, CHIPS)] + [other]
    for dev in peers:
        pl.semaphore_signal(barrier, inc=1, device_id=dev, device_id_type=MESH)
    pl.semaphore_wait(barrier, len(peers))

    def first_row(t, core):
        return core * 4 * SUBS[t] + t * 2 * MAIN

    def piece(ref, slots, t, a, b):
        rows = pl.ds(pl.multiple_of(first_row(t, c) + b * SUBS[t], 16), SUBS[t])
        cols = pl.ds(pl.multiple_of(a * (Q_ALL // 4), TILE), Q_ALL // 4)
        return ref.at[rows, cols] if slots is None else ref.at[slots, rows, cols]

    for s in (1, 3, 2):
        i = SLOT_OF[4 - s]
        for t in range(2):
            send(
                piece(weight, None, t, pa[t], pb[t]), piece(wbuf, i, t, pa[t], pb[t]),
                w_s.at[0], y_r.at[t, i], at_y(s),
            )

    def choose(table, s, out):
        first = ((mod(f + s, 4) * 16 + e) * 2 + o) * TILES
        for k in range(TILES):
            out[pl.ds(k * RANK, RANK), :] = table[lax.rem(lang[first + k], LANGS)]

    loads[2].wait()
    own = ((f * 16 + e) * 2 + o) * TILES
    slot = iota((TILE, Q_ALL), 0)
    for k in range(TILES):
        rows = pl.ds(k * TILE, TILE)
        og[rows, :] = jnp.where(slot < live[own + k], og[rows, :].astype(jnp.float32), 0.0).astype(jnp.bfloat16)

    groups = ((pl.ds(0, 2), (0, 1)), (pl.ds(2, 1), (2,)))
    every = pl.ds(0, 3)

    def b_sends(t, s):
        unit = piece(wbuf, every, t, mod(pa[t] - s, 4), pb[t])
        send(unit, unit, w_s.at[0], b_r.at[t, 0, s], at_ab(t, 0, 1))
        send(unit, unit, w_s.at[0], b_r.at[t, 1, s], at_ab(t, 0, -1))

    for g in range(2):
        for t in range(2):
            for i in groups[g][1]:
                await_ref(piece(wbuf, i, t, pa[t], pb[t]), y_r.at[t, i])
            unit = piece(wbuf, groups[g][0], t, pa[t], pb[t])
            for s in (2, 1, 3):
                send(unit, unit, w_s.at[0], a_r.at[t, s - 1, g], at_ab(t, s, 0))
        if g == 0:
            loads[0].wait()
            for s in (2, 1, 3):
                choose(auv, s, su.at[s - 1])
                send(su.at[s - 1], uu.at[f], u_s.at[0], u_r.at[0], at_y(s))

    choose(auv, 0, uu.at[f])
    n = iota((T, T), 1)
    chip, y, k = lax.div(n, 64), lax.rem(lax.div(n, 16), 4), lax.rem(lax.div(n, 4), 4)
    source = one_hot(iota((T, T), 0) == ((y * 16 + chip * 2 + c) * 2 + o) * TILES + k)
    langs = jnp.broadcast_to(lang_row[...].astype(jnp.float32), (16, T)).astype(jnp.bfloat16)
    langs = dot(langs, source)[:1]
    m, n = iota((ROWS, T), 0), iota((ROWS, T), 1)
    wanted = (lax.div(m, 4) + o * LANGS).astype(jnp.float32)
    pick[...] = one_hot((langs == wanted) & (lax.rem(n, 4) == lax.rem(m, 4)))

    j, t = iota((ROWS, T), 0), iota((ROWS, T), 1)
    limit = jnp.where(
        t < 2 * TILE,
        jnp.where(t < TILE, live[own], live[own + 1]),
        jnp.where(t < 3 * TILE, live[own + 2], live[own + 3]),
    )
    mask = (lax.div(j, RANK) == lax.div(t, TILE)) & (lax.rem(t, TILE) < limit)
    perm_t = permutation((ROWS, ROWS)).astype(jnp.float32).T.astype(jnp.bfloat16)

    def rows_by_chip(v):
        v = jnp.where(mask, v, 0.0).astype(jnp.bfloat16)
        return dot(perm_t, v).astype(jnp.bfloat16)

    await_ref(uu.at[pl.ds(0, 3)], u_r.at[0])
    for t in range(2):
        b_sends(t, 0)
    bt = jnp.zeros((ROWS, T), jnp.float32)
    bb = jnp.zeros((T, ROWS), jnp.float32)
    for y in range(YN):
        bt += dot(uu[y], og[:, y * Q_SH : (y + 1) * Q_SH], NT)
        bb += dot(og[:, y * Q_SH : (y + 1) * Q_SH], uu[y], NT)
    tt, jj = iota((T, ROWS), 0), iota((T, ROWS), 1)
    bb = jnp.where(lax.div(jj, RANK) == lax.div(tt, TILE), bb, 0.0).astype(jnp.bfloat16)
    b2[...] = (bb.astype(jnp.float32) * 2.0).astype(jnp.bfloat16)
    btp[...] = rows_by_chip(bt)

    loads[3].wait()
    for s in (2, 1, 3, 0):
        y = mod(f + s, 4)
        part = dot(btp[...], tok[:, pl.ds(pl.multiple_of(y * D_SH, TILE), D_SH)]).astype(jnp.bfloat16)
        if s:
            spd[s - 1] = part
            send(spd.at[s - 1], r1d.at[f], pd_s.at[0], pd_r.at[0], at_y(s))
        else:
            r1d[f] = part

    loads[1].wait()
    for s in (2, 1, 3):
        choose(adv, s, sd.at[s - 1])
        send(sd.at[s - 1], dd.at[f], d_s.at[0], d_r.at[0], at_y(s))
    choose(adv, 0, dd.at[f])

    def spread(r1, r2, s, ssem, rsem):
        y = mod(f - s, 4)

        def one(i, _):
            chip = lax.rem(q + i, CHIPS)
            rcopy(
                r1.at[y, pl.ds(pl.multiple_of(chip * 16, 16), 16)], r2.at[q, y],
                ssem, rsem, at_chip(chip),
            ).start()
            return 0

        lax.fori_loop(1, CHIPS, one, 0)
        pltpu.make_async_copy(r1.at[y, pl.ds(pl.multiple_of(q * 16, 16), 16)], r2.at[q, y], rsem).start()

    spread(r1d, r2d, 0, xd_s.at[0], xd_r.at[0])

    for s in (1, 3, 2):
        for t in range(2):
            for g in range(2):
                await_ref(piece(wbuf, groups[g][0], t, mod(pa[t] - s, 4), pb[t]), a_r.at[t, s - 1, g])
            b_sends(t, s)

    def block(t, rel):
        rows = pl.ds(pl.multiple_of(first_row(t, c) + mod(pb[t] + rel, 4) * SUBS[t], 16), SUBS[t])
        return wbuf.at[:, rows]

    def block_to_other(t, rel):
        send(block(t, rel), block(t, rel), w_s.at[0], c_r.at[t], other)

    def block_arrived(t):
        await_ref(block(t, 2), f_r.at[t])

    block_to_other(0, 0)

    def way_of(t, s):
        return (1 - swap[t]) * (2 * lax.rem(z, 2) - 1) + swap[t] * (1 if s in (0, 2) else -1)

    def pass_on(t, s):
        way = way_of(t, s)
        unit = piece(wbuf, every, t, mod(pa[t] - s, 4), mod(pb[t] - way, 4))
        await_ref(unit, b_r.at[t, lax.div(1 - way, 2), s])
        send(unit, unit, w_s.at[0], f_r.at[t], at_ab(t, 0, way))

    def rest(t, s):
        way = way_of(t, s)
        await_ref(piece(wbuf, every, t, mod(pa[t] - s, 4), mod(pb[t] + way, 4)), b_r.at[t, lax.div(1 + way, 2), s])

    pass_on(0, 0)

    def columns(w, y, first, width):
        d = dd[y, :, pl.ds(first, width)]
        value = (dot(og[...], w, NT) + dot(b2[...], d)).astype(jnp.bfloat16)
        ig[:, pl.ds(pl.multiple_of(y * D_SH + first, TILE), width)] = value

    loads[4].wait()

    def local_chunk(i, _):
        first = pl.multiple_of(i * LOCAL, TILE)
        columns(wl[pl.ds(first, LOCAL), :], f, first, LOCAL)
        return 0

    lax.fori_loop(0, D_SH // LOCAL, local_chunk, 0)

    def gathered(i, core):
        first = pl.multiple_of(core * MAIN, TILE)
        columns(wbuf[i, pl.ds(first, MAIN), :], mod(f + SLOTS[i], 4), first, MAIN)

    def spread_down(s):
        spread(r1d, r2d, s, xd_s.at[0], xd_r.at[0])

    def spread_up(s):
        spread(r1u, r2u, s, xu_s.at[0], xu_r.at[0])

    await_ref(r1d.at[pl.ds(0, 3)], pd_r.at[0])
    for s in (1, 3, 2):
        spread_down(s)
    for s in (1, 3, 2):
        pass_on(0, s)
    for s in range(4):
        rest(0, s)
    for rel in (1, 3):
        block_to_other(0, rel)
    await_ref(dd.at[pl.ds(0, 3)], d_r.at[0])
    ht = jnp.zeros((ROWS, T), jnp.float32)
    for y in range(YN):
        ht += dot(dd[y], tok[:, y * D_SH : (y + 1) * D_SH], NT)
    htp[...] = rows_by_chip(ht)
    for s in (2, 1, 3, 0):
        y = mod(f + s, 4)
        part = dot(htp[...], og[:, pl.ds(pl.multiple_of(y * Q_SH, TILE), Q_SH)]).astype(jnp.bfloat16)
        if s:
            spu[s - 1] = part
            send(spu.at[s - 1], r1u.at[f], pu_s.at[0], pu_r.at[0], at_y(s))
        else:
            r1u[f] = part
    spread(r1u, r2u, 0, xu_s.at[0], xu_r.at[0])

    def tail_rows(i, late):
        half = (1 - i) * (1 - late) + i * late
        return pl.ds(pl.multiple_of(2 * HALF + c * MINE + half * (MINE // 2), 16), MINE // 2)

    def tail_sends(late):
        for i, s in ((1, 1), (0, 3)):
            rows = tail_rows(i, late)
            send(weight.at[rows], wbuf.at[i, rows], w_s.at[0], t_r.at[i, late], at_y(s))

    tail_sends(0)
    tail_sends(1)

    for s in (0, 1, 3, 2):
        pass_on(1, s)
    block_arrived(0)
    block_to_other(0, 2)

    scale = 2.0 / 256.0

    def send_sum(width):
        part, there = xout.at[:, pl.ds(0, width)], xin.at[:, pl.ds(0, width)]
        return rcopy(part, there, xc_s.at[0], xc_r.at[0], other)

    def place(dz, s, r):
        return gg.at[chip_of(dz, s), :, pl.ds(*PARTS[r])]

    def mine(r):
        return gv.at[:, pl.ds(PARTS[r][0] - (D_SH if r > 1 else 0), PARTS[r][1])]

    def to_x(src, dst, r, k):
        for s in (2, 1, 3):
            rcopy(src, dst, g_s.at[0], g_r.at[r % 2, k + s - 1], at_chip(chip_of(0, -s))).start()

    def to_z(src, dst, r, k):
        rcopy(src, dst, g_s.at[0], g_r.at[r % 2, k], at_chip(chip_of(1, 0))).start()

    def to_core(src, dst, r, k):
        rcopy(src, dst, e_s.at[0], e_r.at[0], other).start()

    def start_gather(r):
        to_z(mine(r + 1), place(0, 0, r + 1), r + 1, 3)
        to_x(mine(r), place(0, 0, r), r, 0)
        to_x(mine(r + 1), place(0, 0, r + 1), r + 1, 0)
        to_z(mine(r), place(0, 0, r), r, 3)
        for h in (r, r + 1):
            to_core(mine(h), place(0, 0, h), h, 0)
            pltpu.make_async_copy(mine(h), place(0, 0, h), own_s.at[0]).start()

    def turn(r):
        part = hand_over(1, 0, r + 1)
        to_x(part, part, r + 1, 4)
        for s in (1, 3, 2):
            part = hand_over(0, s, r)
            to_z(part, part, r, 3 + s)

    def last_hop(r):
        for dz in (0, 1):
            for s in (1, 3, 2):
                hand_over(dz, s, r + 1)
        for s in (0, 1, 3, 2):
            hand_over(1, s, r)

    def hand_over(dz, s, r):
        part = place(dz, s, r)
        await_ref(part, g_r.at[r % 2, s - 1 if dz == 0 else 3 + s])
        to_core(part, part, r, dz * 4 + s)
        return part

    await_ref(r2d, xd_r.at[0])
    down = dot(pick[...], r2d[...].reshape(T, D_SH))

    @pl.when(c == 1)
    def _():
        xout[...] = down
        send_sum(D_SH).start()

    gathered(0, c)
    gathered(1, c)
    await_ref(r1u.at[pl.ds(0, 3)], pu_r.at[0])
    for s in (1, 3, 2):
        spread_up(s)

    @pl.when(c == 0)
    def _():
        await_ref(xin, xc_r.at[0])
        gv[...] = ((down + xin[...]) * scale).astype(jnp.bfloat16)
        start_gather(0)

    gathered(2, c)
    await_ref(r2u, xu_r.at[0])
    up = dot(pick[...], r2u[...].reshape(T, Q_SH))

    @pl.when(c == 0)
    def _():
        xout[:, :Q_SH] = up
        send_sum(Q_SH).start()

    for i, s in ((1, 1), (0, 3)):
        rows = tail_rows(i, 0)
        await_ref(wbuf.at[i, rows], t_r.at[i, 0])
        send(wbuf.at[i, rows], wbuf.at[2, rows], w_s.at[0], tf_r.at[i], at_y(s))

    @pl.when(c == 1)
    def _():
        await_ref(xin.at[:, pl.ds(0, Q_SH)], xc_r.at[0])
        gv[:, :Q_SH] = ((up + xin[:, :Q_SH]) * scale).astype(jnp.bfloat16)
        start_gather(2)

    def from_other(t):
        rows = pl.ds(pl.multiple_of(first_row(t, 1 - c), 16), 4 * SUBS[t])
        await_ref(wbuf.at[:, rows], c_r.at[t])

    from_other(0)
    gathered(0, 1 - c)

    @pl.when(c == 0)
    def _():
        turn(0)

    gathered(1, 1 - c)
    mine_rows = pl.ds(pl.multiple_of(2 * HALF + c * MINE, 16), MINE)
    theirs = pl.ds(pl.multiple_of(2 * HALF + (1 - c) * MINE, 16), MINE)
    for i in range(2):
        await_ref(wbuf.at[i, tail_rows(i, 1)], t_r.at[i, 1])
    near = wbuf.at[pl.ds(0, 2), mine_rows]
    send(near, near, w_s.at[0], tc_r.at[0], other)
    for s in range(4):
        rest(1, s)
    block_arrived(1)
    for rel in range(4):
        block_to_other(1, rel)

    @pl.when(c == 1)
    def _():
        turn(2)

    gathered(2, 1 - c)

    from_other(1)
    await_ref(wbuf.at[pl.ds(0, 2), theirs], tc_r.at[0])
    last = D_SH - 2 * MAIN
    near_sum = dot(og[...], wbuf[0:2, 2 * MAIN :, :].reshape(2 * last, Q_ALL), NT)
    for i in range(2):
        y = mod(f + SLOTS[i], 4)
        value = near_sum[:, i * last : (i + 1) * last] + dot(b2[...], dd[y, :, 2 * MAIN :])
        ig[:, pl.ds(pl.multiple_of(y * D_SH + 2 * MAIN, TILE), last)] = value.astype(jnp.bfloat16)
    for i in range(2):
        await_ref(wbuf.at[2, tail_rows(i, 0)], tf_r.at[i])
    far = wbuf.at[2, mine_rows]
    send(far, far, w_s.at[0], tc_r.at[1], other)

    @pl.when(c == 0)
    def _():
        last_hop(0)

    @pl.when(c == 1)
    def _():
        last_hop(2)

    await_ref(wbuf.at[2, theirs], tc_r.at[1])
    columns(wbuf[2, 2 * MAIN :, :], mod(f + SLOTS[2], 4), 2 * MAIN, last)

    def finish(width, first):
        ours, theirs = pl.ds(first, width), pl.ds(D_SH - first, G_ALL - width)
        await_ref(gg.at[:, :, theirs], e_r.at[0])
        send_sum(G_ALL - width).wait_send()
        await_ref(gv.at[:, pl.ds(0, width)], own_s.at[0])
        await_ref(gg.at[pl.ds(0, CHIPS - 1), :, ours], g_s.at[0])
        await_ref(gg.at[:, :, ours], e_s.at[0])

    @pl.when(c == 0)
    def _():
        finish(D_SH, 0)

    @pl.when(c == 1)
    def _():
        finish(Q_SH, D_SH)

    await_ref(wbuf, w_s.at[0])
    for ref, ssem in ((su, u_s), (sd, d_s), (spd, pd_s), (spu, pu_s)):
        await_ref(ref, ssem.at[0])
    for r1, ssem in ((r1d, xd_s), (r1u, xu_s)):
        await_ref(r1.at[:, pl.ds(0, 16 * (CHIPS - 1))], ssem.at[0])


def finish_kernel(gg, ig_in, down, up, ig, dv, uv, out_s):
    outs = []

    def emit(src, dst, i, g):
        cp = pltpu.make_async_copy(src, dst, out_s.at[i, g])
        cp.start()
        outs.append(cp)

    for g in range(4):
        rows = pl.ds(g * TILE, TILE)
        emit(ig_in.at[rows], ig.at[rows], 2, g)
    perm = permutation((ROWS, ROWS))
    for g in range(4):
        for h in (2 * g, 2 * g + 1):
            rows = gg[:, h * 16 : (h + 1) * 16, :].reshape(ROWS, G_ALL)
            rows = dot(perm, rows).astype(jnp.bfloat16).reshape(4, RANK, G_ALL)
            dv[h * 4 : (h + 1) * 4] = rows[:, :, :D_SH]
            uv[h * 4 : (h + 1) * 4] = rows[:, :, D_SH:]
        part = pl.ds(g * 8, 8)
        emit(dv.at[part], down.at[part], 0, g)
        emit(uv.at[part], up.at[part], 1, g)
    for cp in outs:
        cp.wait()


def on_device(tokens, output_gradient, tile_language, tile_live_count, frozen_weight, adapter_down, adapter_up):
    bf = jnp.bfloat16
    pin = pltpu.with_memory_space_constraint
    tokens, output_gradient, frozen_weight, adapter_down, adapter_up = (
        pin(a, pltpu.HBM) for a in (tokens, output_gradient, frozen_weight, adapter_down, adapter_up)
    )
    hbm, smem, vmem = (pl.BlockSpec(memory_space=s) for s in (pl.ANY, pltpu.SMEM, pltpu.VMEM))
    sem = pltpu.SemaphoreType.DMA

    def sems(*shapes):
        return [sem(s) for s in shapes]

    def buf(*shape, dtype=bf):
        return pltpu.VMEM(shape, dtype)

    ig, gg = pl.pallas_call(
        main_kernel,
        out_shape=(
            buf(T, D_ALL),
            buf(CHIPS, ROWS, G_ALL),
        ),
        in_specs=[smem, smem, vmem, hbm, hbm, hbm, hbm, hbm],
        out_specs=(vmem, vmem),
        scratch_shapes=[
            buf(3, D_SH, Q_ALL),
            buf(D_SH, Q_ALL),
            buf(T, D_ALL),
            buf(T, Q_ALL),
            buf(LANGS, RANK, D_SH),
            buf(LANGS, RANK, Q_SH),
            buf(3, ROWS, Q_SH),
            buf(3, ROWS, D_SH),
            buf(YN, ROWS, Q_SH),
            buf(YN, ROWS, D_SH),
            buf(3, ROWS, D_SH),
            buf(3, ROWS, Q_SH),
            buf(YN, ROWS, D_SH),
            buf(YN, ROWS, Q_SH),
            buf(CHIPS, YN, 16, D_SH),
            buf(CHIPS, YN, 16, Q_SH),
            buf(ROWS, D_SH, dtype=jnp.float32),
            buf(ROWS, D_SH, dtype=jnp.float32),
            buf(ROWS, D_SH),
            buf(T, ROWS),
            buf(ROWS, T),
            buf(ROWS, T),
            buf(ROWS, T),
            *sems((5,), (1,), (2, 3), (2, 3, 2), (2, 2, 4), (2,), (2,), (2, 2), (2,), (2,)),
            *sems(*[(1,)] * 8, *[(1,)] * 4, (1,), (1,), (1,), (2, 7), (1,), (1,), (1,)),
        ],
        compiler_params=pltpu.CompilerParams(
            collective_id=0, has_side_effects=True, vmem_limit_bytes=46 * 2**20
        ),
        cost_estimate=pl.CostEstimate(flops=12 * 10**9, bytes_accessed=40 * 10**6, transcendentals=0),
        name="exchange",
    )(
        pin(tile_language, pltpu.HBM), pin(tile_live_count, pltpu.HBM), tile_language.reshape(1, T),
        tokens, output_gradient, frozen_weight, adapter_down, adapter_up,
    )
    down, up, ig = pl.pallas_call(
        finish_kernel,
        out_shape=(
            jax.ShapeDtypeStruct((LANGS, RANK, D_SH), bf),
            jax.ShapeDtypeStruct((LANGS, RANK, Q_SH), bf),
            jax.ShapeDtypeStruct((T, D_ALL), bf),
        ),
        in_specs=[vmem, vmem],
        out_specs=(hbm, hbm, hbm),
        scratch_shapes=[buf(LANGS, RANK, D_SH), buf(LANGS, RANK, Q_SH), sem((3, 4))],
        compiler_params=pltpu.CompilerParams(vmem_limit_bytes=16 * 2**20),
        name="finish",
    )(pin(gg, pltpu.VMEM), pin(ig, pltpu.VMEM))
    return ig, down, up


def solution(mesh):
    tok = P(("fsdp", "dp", "owner"), None)
    adapter = P("owner", None, "fsdp")
    return jax.shard_map(
        on_device,
        mesh=mesh,
        in_specs=(tok, tok, P(), P(), P("fsdp", None), adapter, adapter),
        out_specs=(tok, adapter, adapter),
        check_vma=False,
    )
```

```python
import functools

import jax
import jax.numpy as jnp
from jax import lax
from jax.experimental import pallas as pl
from jax.experimental.pallas import tpu as pltpu
from jax.sharding import PartitionSpec as P

MESH = pl.DeviceIdType.MESH
NT = (((1,), (1,)), ((), ()))
NN = (((1,), (0,)), ((), ()))

TILE = 128
TILES = 4
RANK = 32
ROWS = TILES * RANK
LANGS = 32
YN = 4
CHIPS = 8
T = TILE * TILES
D_ALL, Q_ALL = 4608, 2048
D_SH, Q_SH = D_ALL // YN, Q_ALL // YN
G_ALL = D_SH + Q_SH
SUBS = (96, 16)
MAIN = 4 * SUBS[0]
HALF = 4 * sum(SUBS)
TAIL = D_SH - 2 * HALF
MINE = TAIL // 2
LOCAL = 384
SLOTS = (1, 3, 2)
SLOT_OF = {1: 0, 3: 1, 2: 2}
PARTS = ((0, 640), (640, 512), (D_SH, 256), (D_SH + 256, 256))


def dot(a, b, dims=NN):
    return lax.dot_general(a, b, dims, preferred_element_type=jnp.float32)


def one_hot(cond):
    return cond.astype(jnp.float32).astype(jnp.bfloat16)


def iota(shape, dim):
    return lax.broadcasted_iota(jnp.int32, shape, dim)


def permutation(shape):
    i, j = iota(shape, 0), iota(shape, 1)
    k, q, r = lax.div(lax.rem(j, 16), 4), lax.div(j, 16), lax.rem(j, 4)
    return one_hot(i == k * RANK + q * 4 + r)


def main_kernel(
    lang, live, lang_row, tokens, grad, weight, adown, aup,
    ig, gg,
    wbuf, wl, tok, og, adv, auv, su, sd, uu, dd, spd, spu, r1d, r1u, r2d, r2u, xout, xin, gv, b2, btp, htp, pick,
    in_sem, w_s, y_r, a_r, b_r, f_r, c_r, t_r, tf_r, tc_r,
    u_s, u_r, d_s, d_r, pd_s, pd_r, pu_s, pu_r, xd_s, xd_r, xu_s, xu_r, xc_s, xc_r, g_s, g_r, e_s, e_r, own_s,
):
    f, e, o = lax.axis_index("fsdp"), lax.axis_index("dp"), lax.axis_index("owner")
    q, c = lax.div(e, 2), lax.rem(e, 2)
    x, zl = lax.rem(q, 4), lax.div(q, 4)
    z = o * 2 + zl
    pa = (x * (1 - c) + z * c, x)
    pb = (z * (1 - c) + x * c, z)
    swap = (c, 0)

    def mod(v, n):
        return lax.rem(v + n, n)

    def at_ab(t, da, db):
        a, b = mod(pa[t] + da, 4), mod(pb[t] + db, 4)
        xx, zz = a * (1 - swap[t]) + b * swap[t], b * (1 - swap[t]) + a * swap[t]
        return (f, lax.rem(zz, 2) * 8 + xx * 2 + c, lax.div(zz, 2))

    def at_y(s):
        return (mod(f + s, 4), e, o)

    def at_chip(chip):
        return (f, chip * 2 + c, o)

    def chip_of(dz, s):
        return lax.rem(zl + dz, 2) * 4 + mod(x - s, 4)

    other = (f, q * 2 + 1 - c, o)

    def rcopy(src, dst, ssem, rsem, dev):
        return pltpu.make_async_remote_copy(
            src_ref=src, dst_ref=dst, send_sem=ssem, recv_sem=rsem, device_id=dev, device_id_type=MESH
        )

    def await_ref(ref, sem):
        pltpu.make_async_copy(ref, ref, sem).wait()

    def send(*args):
        rcopy(*args).start()

    loads = [
        pltpu.make_async_copy(s, d, in_sem.at[i])
        for i, (s, d) in enumerate(((aup, auv), (adown, adv), (grad, og), (tokens, tok), (weight, wl)))
    ]
    for cp in loads:
        cp.start()

    barrier = pltpu.get_barrier_semaphore()
    peers = [at_y(s) for s in (1, 2, 3)]
    for t in range(2):
        peers += [at_ab(t, s, 0) for s in (1, 2, 3)] + [at_ab(t, 0, 1), at_ab(t, 0, -1)]
    peers += [at_chip(lax.rem(q + s, CHIPS)) for s in range(1, CHIPS)] + [other]
    for dev in peers:
        pl.semaphore_signal(barrier, inc=1, device_id=dev, device_id_type=MESH)
    pl.semaphore_wait(barrier, len(peers))

    def first_row(t, core):
        return core * 4 * SUBS[t] + t * 2 * MAIN

    def piece(ref, slots, t, a, b):
        rows = pl.ds(pl.multiple_of(first_row(t, c) + b * SUBS[t], 16), SUBS[t])
        cols = pl.ds(pl.multiple_of(a * (Q_ALL // 4), TILE), Q_ALL // 4)
        return ref.at[rows, cols] if slots is None else ref.at[slots, rows, cols]

    for s in (1, 3, 2):
        i = SLOT_OF[4 - s]
        for t in range(2):
            send(
                piece(weight, None, t, pa[t], pb[t]), piece(wbuf, i, t, pa[t], pb[t]),
                w_s.at[0], y_r.at[t, i], at_y(s),
            )

    def choose(table, s, out):
        first = ((mod(f + s, 4) * 16 + e) * 2 + o) * TILES
        for k in range(TILES):
            out[pl.ds(k * RANK, RANK), :] = table[lax.rem(lang[first + k], LANGS)]

    loads[2].wait()
    own = ((f * 16 + e) * 2 + o) * TILES
    slot = iota((TILE, Q_ALL), 0)
    for k in range(TILES):
        rows = pl.ds(k * TILE, TILE)
        og[rows, :] = jnp.where(slot < live[own + k], og[rows, :].astype(jnp.float32), 0.0).astype(jnp.bfloat16)

    groups = ((pl.ds(0, 2), (0, 1)), (pl.ds(2, 1), (2,)))
    every = pl.ds(0, 3)

    def b_sends(t, s):
        unit = piece(wbuf, every, t, mod(pa[t] - s, 4), pb[t])
        send(unit, unit, w_s.at[0], b_r.at[t, 0, s], at_ab(t, 0, 1))
        send(unit, unit, w_s.at[0], b_r.at[t, 1, s], at_ab(t, 0, -1))

    for g in range(2):
        for t in range(2):
            for i in groups[g][1]:
                await_ref(piece(wbuf, i, t, pa[t], pb[t]), y_r.at[t, i])
            unit = piece(wbuf, groups[g][0], t, pa[t], pb[t])
            for s in (2, 1, 3):
                send(unit, unit, w_s.at[0], a_r.at[t, s - 1, g], at_ab(t, s, 0))
        if g == 0:
            loads[0].wait()
            for s in (2, 1, 3):
                choose(auv, s, su.at[s - 1])
                send(su.at[s - 1], uu.at[f], u_s.at[0], u_r.at[0], at_y(s))

    choose(auv, 0, uu.at[f])
    n = iota((T, T), 1)
    chip, y, k = lax.div(n, 64), lax.rem(lax.div(n, 16), 4), lax.rem(lax.div(n, 4), 4)
    source = one_hot(iota((T, T), 0) == ((y * 16 + chip * 2 + c) * 2 + o) * TILES + k)
    langs = jnp.broadcast_to(lang_row[...].astype(jnp.float32), (16, T)).astype(jnp.bfloat16)
    langs = dot(langs, source)[:1]
    m, n = iota((ROWS, T), 0), iota((ROWS, T), 1)
    wanted = (lax.div(m, 4) + o * LANGS).astype(jnp.float32)
    pick[...] = one_hot((langs == wanted) & (lax.rem(n, 4) == lax.rem(m, 4)))

    j, t = iota((ROWS, T), 0), iota((ROWS, T), 1)
    limit = jnp.where(
        t < 2 * TILE,
        jnp.where(t < TILE, live[own], live[own + 1]),
        jnp.where(t < 3 * TILE, live[own + 2], live[own + 3]),
    )
    mask = (lax.div(j, RANK) == lax.div(t, TILE)) & (lax.rem(t, TILE) < limit)
    perm_t = permutation((ROWS, ROWS)).astype(jnp.float32).T.astype(jnp.bfloat16)

    def rows_by_chip(v):
        v = jnp.where(mask, v, 0.0).astype(jnp.bfloat16)
        return dot(perm_t, v).astype(jnp.bfloat16)

    await_ref(uu.at[pl.ds(0, 3)], u_r.at[0])
    for t in range(2):
        b_sends(t, 0)
    bt = jnp.zeros((ROWS, T), jnp.float32)
    bb = jnp.zeros((T, ROWS), jnp.float32)
    for y in range(YN):
        bt += dot(uu[y], og[:, y * Q_SH : (y + 1) * Q_SH], NT)
        bb += dot(og[:, y * Q_SH : (y + 1) * Q_SH], uu[y], NT)
    tt, jj = iota((T, ROWS), 0), iota((T, ROWS), 1)
    bb = jnp.where(lax.div(jj, RANK) == lax.div(tt, TILE), bb, 0.0).astype(jnp.bfloat16)
    b2[...] = (bb.astype(jnp.float32) * 2.0).astype(jnp.bfloat16)
    btp[...] = rows_by_chip(bt)

    loads[3].wait()
    for s in (2, 1, 3, 0):
        y = mod(f + s, 4)
        part = dot(btp[...], tok[:, pl.ds(pl.multiple_of(y * D_SH, TILE), D_SH)]).astype(jnp.bfloat16)
        if s:
            spd[s - 1] = part
            send(spd.at[s - 1], r1d.at[f], pd_s.at[0], pd_r.at[0], at_y(s))
        else:
            r1d[f] = part

    loads[1].wait()
    for s in (2, 1, 3):
        choose(adv, s, sd.at[s - 1])
        send(sd.at[s - 1], dd.at[f], d_s.at[0], d_r.at[0], at_y(s))
    choose(adv, 0, dd.at[f])

    def spread(r1, r2, s, ssem, rsem):
        y = mod(f - s, 4)

        def one(i, _):
            chip = lax.rem(q + i, CHIPS)
            rcopy(
                r1.at[y, pl.ds(pl.multiple_of(chip * 16, 16), 16)], r2.at[q, y],
                ssem, rsem, at_chip(chip),
            ).start()
            return 0

        lax.fori_loop(1, CHIPS, one, 0)
        pltpu.make_async_copy(r1.at[y, pl.ds(pl.multiple_of(q * 16, 16), 16)], r2.at[q, y], rsem).start()

    spread(r1d, r2d, 0, xd_s.at[0], xd_r.at[0])

    for s in (1, 3, 2):
        for t in range(2):
            for g in range(2):
                await_ref(piece(wbuf, groups[g][0], t, mod(pa[t] - s, 4), pb[t]), a_r.at[t, s - 1, g])
            b_sends(t, s)

    def block(t, rel):
        rows = pl.ds(pl.multiple_of(first_row(t, c) + mod(pb[t] + rel, 4) * SUBS[t], 16), SUBS[t])
        return wbuf.at[:, rows]

    def block_to_other(t, rel):
        send(block(t, rel), block(t, rel), w_s.at[0], c_r.at[t], other)

    def block_arrived(t):
        await_ref(block(t, 2), f_r.at[t])

    block_to_other(0, 0)

    def way_of(t, s):
        return (1 - swap[t]) * (2 * lax.rem(z, 2) - 1) + swap[t] * (1 if s in (0, 2) else -1)

    def pass_on(t, s):
        way = way_of(t, s)
        unit = piece(wbuf, every, t, mod(pa[t] - s, 4), mod(pb[t] - way, 4))
        await_ref(unit, b_r.at[t, lax.div(1 - way, 2), s])
        send(unit, unit, w_s.at[0], f_r.at[t], at_ab(t, 0, way))

    def rest(t, s):
        way = way_of(t, s)
        await_ref(piece(wbuf, every, t, mod(pa[t] - s, 4), mod(pb[t] + way, 4)), b_r.at[t, lax.div(1 + way, 2), s])

    pass_on(0, 0)

    def columns(w, y, first, width):
        d = dd[y, :, pl.ds(first, width)]
        value = (dot(og[...], w, NT) + dot(b2[...], d)).astype(jnp.bfloat16)
        ig[:, pl.ds(pl.multiple_of(y * D_SH + first, TILE), width)] = value

    loads[4].wait()

    def local_chunk(i, _):
        first = pl.multiple_of(i * LOCAL, TILE)
        columns(wl[pl.ds(first, LOCAL), :], f, first, LOCAL)
        return 0

    lax.fori_loop(0, D_SH // LOCAL, local_chunk, 0)

    def gathered(i, core):
        first = pl.multiple_of(core * MAIN, TILE)
        columns(wbuf[i, pl.ds(first, MAIN), :], mod(f + SLOTS[i], 4), first, MAIN)

    def spread_down(s):
        spread(r1d, r2d, s, xd_s.at[0], xd_r.at[0])

    def spread_up(s):
        spread(r1u, r2u, s, xu_s.at[0], xu_r.at[0])

    await_ref(r1d.at[pl.ds(0, 3)], pd_r.at[0])
    for s in (1, 3, 2):
        spread_down(s)
    for s in (1, 3, 2):
        pass_on(0, s)
    for s in range(4):
        rest(0, s)
    for rel in (1, 3):
        block_to_other(0, rel)
    await_ref(dd.at[pl.ds(0, 3)], d_r.at[0])
    ht = jnp.zeros((ROWS, T), jnp.float32)
    for y in range(YN):
        ht += dot(dd[y], tok[:, y * D_SH : (y + 1) * D_SH], NT)
    htp[...] = rows_by_chip(ht)
    for s in (2, 1, 3, 0):
        y = mod(f + s, 4)
        part = dot(htp[...], og[:, pl.ds(pl.multiple_of(y * Q_SH, TILE), Q_SH)]).astype(jnp.bfloat16)
        if s:
            spu[s - 1] = part
            send(spu.at[s - 1], r1u.at[f], pu_s.at[0], pu_r.at[0], at_y(s))
        else:
            r1u[f] = part
    spread(r1u, r2u, 0, xu_s.at[0], xu_r.at[0])

    def tail_rows(i, late):
        half = (1 - i) * (1 - late) + i * late
        return pl.ds(pl.multiple_of(2 * HALF + c * MINE + half * (MINE // 2), 16), MINE // 2)

    def tail_sends(late):
        for i, s in ((1, 1), (0, 3)):
            rows = tail_rows(i, late)
            send(weight.at[rows], wbuf.at[i, rows], w_s.at[0], t_r.at[i, late], at_y(s))

    tail_sends(0)
    tail_sends(1)

    for s in (0, 1, 3, 2):
        pass_on(1, s)
    block_arrived(0)
    block_to_other(0, 2)

    scale = 2.0 / 256.0

    def send_sum(width):
        part, there = xout.at[:, pl.ds(0, width)], xin.at[:, pl.ds(0, width)]
        return rcopy(part, there, xc_s.at[0], xc_r.at[0], other)

    def place(dz, s, r):
        return gg.at[chip_of(dz, s), :, pl.ds(*PARTS[r])]

    def mine(r):
        return gv.at[:, pl.ds(PARTS[r][0] - (D_SH if r > 1 else 0), PARTS[r][1])]

    def to_x(src, dst, r, k):
        for s in (2, 1, 3):
            rcopy(src, dst, g_s.at[0], g_r.at[r % 2, k + s - 1], at_chip(chip_of(0, -s))).start()

    def to_z(src, dst, r, k):
        rcopy(src, dst, g_s.at[0], g_r.at[r % 2, k], at_chip(chip_of(1, 0))).start()

    def to_core(src, dst, r, k):
        rcopy(src, dst, e_s.at[0], e_r.at[0], other).start()

    def start_gather(r):
        to_z(mine(r + 1), place(0, 0, r + 1), r + 1, 3)
        to_x(mine(r), place(0, 0, r), r, 0)
        to_x(mine(r + 1), place(0, 0, r + 1), r + 1, 0)
        to_z(mine(r), place(0, 0, r), r, 3)
        for h in (r, r + 1):
            to_core(mine(h), place(0, 0, h), h, 0)
            pltpu.make_async_copy(mine(h), place(0, 0, h), own_s.at[0]).start()

    def turn(r):
        part = hand_over(1, 0, r + 1)
        to_x(part, part, r + 1, 4)
        for s in (1, 3, 2):
            part = hand_over(0, s, r)
            to_z(part, part, r, 3 + s)

    def last_hop(r):
        for dz in (0, 1):
            for s in (1, 3, 2):
                hand_over(dz, s, r + 1)
        for s in (0, 1, 3, 2):
            hand_over(1, s, r)

    def hand_over(dz, s, r):
        part = place(dz, s, r)
        await_ref(part, g_r.at[r % 2, s - 1 if dz == 0 else 3 + s])
        to_core(part, part, r, dz * 4 + s)
        return part

    await_ref(r2d, xd_r.at[0])
    down = dot(pick[...], r2d[...].reshape(T, D_SH))

    @pl.when(c == 1)
    def _():
        xout[...] = down
        send_sum(D_SH).start()

    gathered(0, c)
    gathered(1, c)
    await_ref(r1u.at[pl.ds(0, 3)], pu_r.at[0])
    for s in (1, 3, 2):
        spread_up(s)

    @pl.when(c == 0)
    def _():
        await_ref(xin, xc_r.at[0])
        gv[...] = ((down + xin[...]) * scale).astype(jnp.bfloat16)
        start_gather(0)

    gathered(2, c)
    await_ref(r2u, xu_r.at[0])
    up = dot(pick[...], r2u[...].reshape(T, Q_SH))

    @pl.when(c == 0)
    def _():
        xout[:, :Q_SH] = up
        send_sum(Q_SH).start()

    for i, s in ((1, 1), (0, 3)):
        rows = tail_rows(i, 0)
        await_ref(wbuf.at[i, rows], t_r.at[i, 0])
        send(wbuf.at[i, rows], wbuf.at[2, rows], w_s.at[0], tf_r.at[i], at_y(s))

    @pl.when(c == 1)
    def _():
        await_ref(xin.at[:, pl.ds(0, Q_SH)], xc_r.at[0])
        gv[:, :Q_SH] = ((up + xin[:, :Q_SH]) * scale).astype(jnp.bfloat16)
        start_gather(2)

    def from_other(t):
        rows = pl.ds(pl.multiple_of(first_row(t, 1 - c), 16), 4 * SUBS[t])
        await_ref(wbuf.at[:, rows], c_r.at[t])

    from_other(0)
    gathered(0, 1 - c)

    @pl.when(c == 0)
    def _():
        turn(0)

    gathered(1, 1 - c)
    mine_rows = pl.ds(pl.multiple_of(2 * HALF + c * MINE, 16), MINE)
    theirs = pl.ds(pl.multiple_of(2 * HALF + (1 - c) * MINE, 16), MINE)
    for i in range(2):
        await_ref(wbuf.at[i, tail_rows(i, 1)], t_r.at[i, 1])
    near = wbuf.at[pl.ds(0, 2), mine_rows]
    send(near, near, w_s.at[0], tc_r.at[0], other)
    for s in range(4):
        rest(1, s)
    block_arrived(1)
    for rel in range(4):
        block_to_other(1, rel)

    @pl.when(c == 1)
    def _():
        turn(2)

    gathered(2, 1 - c)

    from_other(1)
    await_ref(wbuf.at[pl.ds(0, 2), theirs], tc_r.at[0])
    last = D_SH - 2 * MAIN
    near_sum = dot(og[...], wbuf[0:2, 2 * MAIN :, :].reshape(2 * last, Q_ALL), NT)
    for i in range(2):
        y = mod(f + SLOTS[i], 4)
        value = near_sum[:, i * last : (i + 1) * last] + dot(b2[...], dd[y, :, 2 * MAIN :])
        ig[:, pl.ds(pl.multiple_of(y * D_SH + 2 * MAIN, TILE), last)] = value.astype(jnp.bfloat16)
    for i in range(2):
        await_ref(wbuf.at[2, tail_rows(i, 0)], tf_r.at[i])
    far = wbuf.at[2, mine_rows]
    send(far, far, w_s.at[0], tc_r.at[1], other)

    @pl.when(c == 0)
    def _():
        last_hop(0)

    @pl.when(c == 1)
    def _():
        last_hop(2)

    await_ref(wbuf.at[2, theirs], tc_r.at[1])
    columns(wbuf[2, 2 * MAIN :, :], mod(f + SLOTS[2], 4), 2 * MAIN, last)

    def finish(width, first):
        ours, theirs = pl.ds(first, width), pl.ds(D_SH - first, G_ALL - width)
        await_ref(gg.at[:, :, theirs], e_r.at[0])
        send_sum(G_ALL - width).wait_send()
        await_ref(gv.at[:, pl.ds(0, width)], own_s.at[0])
        await_ref(gg.at[pl.ds(0, CHIPS - 1), :, ours], g_s.at[0])
        await_ref(gg.at[:, :, ours], e_s.at[0])

    @pl.when(c == 0)
    def _():
        finish(D_SH, 0)

    @pl.when(c == 1)
    def _():
        finish(Q_SH, D_SH)

    await_ref(wbuf, w_s.at[0])
    for ref, ssem in ((su, u_s), (sd, d_s), (spd, pd_s), (spu, pu_s)):
        await_ref(ref, ssem.at[0])
    for r1, ssem in ((r1d, xd_s), (r1u, xu_s)):
        await_ref(r1.at[:, pl.ds(0, 16 * (CHIPS - 1))], ssem.at[0])


def finish_kernel(gg, ig_in, down, up, ig, dv, uv, out_s):
    outs = []

    def emit(src, dst, i, g):
        cp = pltpu.make_async_copy(src, dst, out_s.at[i, g])
        cp.start()
        outs.append(cp)

    for g in range(4):
        rows = pl.ds(g * TILE, TILE)
        emit(ig_in.at[rows], ig.at[rows], 2, g)
    perm = permutation((ROWS, ROWS))
    for g in range(4):
        for h in (2 * g, 2 * g + 1):
            rows = gg[:, h * 16 : (h + 1) * 16, :].reshape(ROWS, G_ALL)
            rows = dot(perm, rows).astype(jnp.bfloat16).reshape(4, RANK, G_ALL)
            dv[h * 4 : (h + 1) * 4] = rows[:, :, :D_SH]
            uv[h * 4 : (h + 1) * 4] = rows[:, :, D_SH:]
        part = pl.ds(g * 8, 8)
        emit(dv.at[part], down.at[part], 0, g)
        emit(uv.at[part], up.at[part], 1, g)
    for cp in outs:
        cp.wait()


def on_device(tokens, output_gradient, tile_language, tile_live_count, frozen_weight, adapter_down, adapter_up):
    bf = jnp.bfloat16
    pin = pltpu.with_memory_space_constraint
    tokens, output_gradient, frozen_weight, adapter_down, adapter_up = (
        pin(a, pltpu.HBM) for a in (tokens, output_gradient, frozen_weight, adapter_down, adapter_up)
    )
    hbm, smem, vmem = (pl.BlockSpec(memory_space=s) for s in (pl.ANY, pltpu.SMEM, pltpu.VMEM))
    sem = pltpu.SemaphoreType.DMA

    def sems(*shapes):
        return [sem(s) for s in shapes]

    def buf(*shape, dtype=bf):
        return pltpu.VMEM(shape, dtype)

    ig, gg = pl.pallas_call(
        main_kernel,
        out_shape=(
            buf(T, D_ALL),
            buf(CHIPS, ROWS, G_ALL),
        ),
        in_specs=[smem, smem, vmem, hbm, hbm, hbm, hbm, hbm],
        out_specs=(vmem, vmem),
        scratch_shapes=[
            buf(3, D_SH, Q_ALL),
            buf(D_SH, Q_ALL),
            buf(T, D_ALL),
            buf(T, Q_ALL),
            buf(LANGS, RANK, D_SH),
            buf(LANGS, RANK, Q_SH),
            buf(3, ROWS, Q_SH),
            buf(3, ROWS, D_SH),
            buf(YN, ROWS, Q_SH),
            buf(YN, ROWS, D_SH),
            buf(3, ROWS, D_SH),
            buf(3, ROWS, Q_SH),
            buf(YN, ROWS, D_SH),
            buf(YN, ROWS, Q_SH),
            buf(CHIPS, YN, 16, D_SH),
            buf(CHIPS, YN, 16, Q_SH),
            buf(ROWS, D_SH, dtype=jnp.float32),
            buf(ROWS, D_SH, dtype=jnp.float32),
            buf(ROWS, D_SH),
            buf(T, ROWS),
            buf(ROWS, T),
            buf(ROWS, T),
            buf(ROWS, T),
            *sems((5,), (1,), (2, 3), (2, 3, 2), (2, 2, 4), (2,), (2,), (2, 2), (2,), (2,)),
            *sems(*[(1,)] * 8, *[(1,)] * 4, (1,), (1,), (1,), (2, 7), (1,), (1,), (1,)),
        ],
        compiler_params=pltpu.CompilerParams(
            collective_id=0, has_side_effects=True, vmem_limit_bytes=46 * 2**20
        ),
        cost_estimate=pl.CostEstimate(flops=12 * 10**9, bytes_accessed=40 * 10**6, transcendentals=0),
        name="exchange",
    )(
        pin(tile_language, pltpu.HBM), pin(tile_live_count, pltpu.HBM), tile_language.reshape(1, T),
        tokens, output_gradient, frozen_weight, adapter_down, adapter_up,
    )
    down, up, ig = pl.pallas_call(
        finish_kernel,
        out_shape=(
            jax.ShapeDtypeStruct((LANGS, RANK, D_SH), bf),
            jax.ShapeDtypeStruct((LANGS, RANK, Q_SH), bf),
            jax.ShapeDtypeStruct((T, D_ALL), bf),
        ),
        in_specs=[vmem, vmem],
        out_specs=(hbm, hbm, hbm),
        scratch_shapes=[buf(LANGS, RANK, D_SH), buf(LANGS, RANK, Q_SH), sem((3, 4))],
        compiler_params=pltpu.CompilerParams(vmem_limit_bytes=16 * 2**20),
        name="finish",
    )(pin(gg, pltpu.VMEM), pin(ig, pltpu.VMEM))
    return ig, down, up


def solution(mesh):
    tok = P(("fsdp", "dp", "owner"), None)
    adapter = P("owner", None, "fsdp")
    return jax.shard_map(
        on_device,
        mesh=mesh,
        in_specs=(tok, tok, P(), P(), P("fsdp", None), adapter, adapter),
        out_specs=(tok, adapter, adapter),
        check_vma=False,
    )
```

```python
import functools

import jax
import jax.numpy as jnp
from jax import lax
from jax.experimental import pallas as pl
from jax.experimental.pallas import tpu as pltpu
from jax.sharding import PartitionSpec as P

MESH = pl.DeviceIdType.MESH
NT = (((1,), (1,)), ((), ()))
NN = (((1,), (0,)), ((), ()))

TILE = 128
TILES = 4
RANK = 32
ROWS = TILES * RANK
LANGS = 32
YN = 4
CHIPS = 8
T = TILE * TILES
D_ALL, Q_ALL = 4608, 2048
D_SH, Q_SH = D_ALL // YN, Q_ALL // YN
G_ALL = D_SH + Q_SH
SUBS = (96, 16)
MAIN = 4 * SUBS[0]
HALF = 4 * sum(SUBS)
TAIL = D_SH - 2 * HALF
MINE = TAIL // 2
LOCAL = 384
SLOTS = (1, 3, 2)
SLOT_OF = {1: 0, 3: 1, 2: 2}
PARTS = ((0, 640), (640, 512), (D_SH, 256), (D_SH + 256, 256))


def dot(a, b, dims=NN):
    return lax.dot_general(a, b, dims, preferred_element_type=jnp.float32)


def one_hot(cond):
    return cond.astype(jnp.float32).astype(jnp.bfloat16)


def iota(shape, dim):
    return lax.broadcasted_iota(jnp.int32, shape, dim)


def permutation(shape):
    i, j = iota(shape, 0), iota(shape, 1)
    k, q, r = lax.div(lax.rem(j, 16), 4), lax.div(j, 16), lax.rem(j, 4)
    return one_hot(i == k * RANK + q * 4 + r)


def main_kernel(
    lang, live, lang_row, tokens, grad, weight, adown, aup,
    ig, gg,
    wbuf, wl, tok, og, adv, auv, su, sd, uu, dd, spd, spu, r1d, r1u, r2d, r2u, xout, xin, gv, b2, btp, htp, pick,
    in_sem, w_s, y_r, a_r, b_r, f_r, c_r, t_r, tf_r, tc_r,
    u_s, u_r, d_s, d_r, pd_s, pd_r, pu_s, pu_r, xd_s, xd_r, xu_s, xu_r, xc_s, xc_r, g_s, g_r, e_s, e_r, own_s,
):
    f, e, o = lax.axis_index("fsdp"), lax.axis_index("dp"), lax.axis_index("owner")
    q, c = lax.div(e, 2), lax.rem(e, 2)
    x, zl = lax.rem(q, 4), lax.div(q, 4)
    z = o * 2 + zl
    pa = (x * (1 - c) + z * c, x)
    pb = (z * (1 - c) + x * c, z)
    swap = (c, 0)

    def mod(v, n):
        return lax.rem(v + n, n)

    def at_ab(t, da, db):
        a, b = mod(pa[t] + da, 4), mod(pb[t] + db, 4)
        xx, zz = a * (1 - swap[t]) + b * swap[t], b * (1 - swap[t]) + a * swap[t]
        return (f, lax.rem(zz, 2) * 8 + xx * 2 + c, lax.div(zz, 2))

    def at_y(s):
        return (mod(f + s, 4), e, o)

    def at_chip(chip):
        return (f, chip * 2 + c, o)

    def chip_of(dz, s):
        return lax.rem(zl + dz, 2) * 4 + mod(x - s, 4)

    other = (f, q * 2 + 1 - c, o)

    def rcopy(src, dst, ssem, rsem, dev):
        return pltpu.make_async_remote_copy(
            src_ref=src, dst_ref=dst, send_sem=ssem, recv_sem=rsem, device_id=dev, device_id_type=MESH
        )

    def await_ref(ref, sem):
        pltpu.make_async_copy(ref, ref, sem).wait()

    def send(*args):
        rcopy(*args).start()

    loads = [
        pltpu.make_async_copy(s, d, in_sem.at[i])
        for i, (s, d) in enumerate(((aup, auv), (adown, adv), (grad, og), (tokens, tok), (weight, wl)))
    ]
    for cp in loads:
        cp.start()

    barrier = pltpu.get_barrier_semaphore()
    peers = [at_y(s) for s in (1, 2, 3)]
    for t in range(2):
        peers += [at_ab(t, s, 0) for s in (1, 2, 3)] + [at_ab(t, 0, 1), at_ab(t, 0, -1)]
    peers += [at_chip(lax.rem(q + s, CHIPS)) for s in range(1, CHIPS)] + [other]
    for dev in peers:
        pl.semaphore_signal(barrier, inc=1, device_id=dev, device_id_type=MESH)
    pl.semaphore_wait(barrier, len(peers))

    def first_row(t, core):
        return core * 4 * SUBS[t] + t * 2 * MAIN

    def piece(ref, slots, t, a, b):
        rows = pl.ds(pl.multiple_of(first_row(t, c) + b * SUBS[t], 16), SUBS[t])
        cols = pl.ds(pl.multiple_of(a * (Q_ALL // 4), TILE), Q_ALL // 4)
        return ref.at[rows, cols] if slots is None else ref.at[slots, rows, cols]

    for s in (1, 3, 2):
        i = SLOT_OF[4 - s]
        for t in range(2):
            send(
                piece(weight, None, t, pa[t], pb[t]), piece(wbuf, i, t, pa[t], pb[t]),
                w_s.at[0], y_r.at[t, i], at_y(s),
            )

    def choose(table, s, out):
        first = ((mod(f + s, 4) * 16 + e) * 2 + o) * TILES
        for k in range(TILES):
            out[pl.ds(k * RANK, RANK), :] = table[lax.rem(lang[first + k], LANGS)]

    loads[2].wait()
    own = ((f * 16 + e) * 2 + o) * TILES
    slot = iota((TILE, Q_ALL), 0)
    for k in range(TILES):
        rows = pl.ds(k * TILE, TILE)
        og[rows, :] = jnp.where(slot < live[own + k], og[rows, :].astype(jnp.float32), 0.0).astype(jnp.bfloat16)

    groups = ((pl.ds(0, 2), (0, 1)), (pl.ds(2, 1), (2,)))
    every = pl.ds(0, 3)

    def b_sends(t, s):
        unit = piece(wbuf, every, t, mod(pa[t] - s, 4), pb[t])
        send(unit, unit, w_s.at[0], b_r.at[t, 0, s], at_ab(t, 0, 1))
        send(unit, unit, w_s.at[0], b_r.at[t, 1, s], at_ab(t, 0, -1))

    for g in range(2):
        for t in range(2):
            for i in groups[g][1]:
                await_ref(piece(wbuf, i, t, pa[t], pb[t]), y_r.at[t, i])
            unit = piece(wbuf, groups[g][0], t, pa[t], pb[t])
            for s in (2, 1, 3):
                send(unit, unit, w_s.at[0], a_r.at[t, s - 1, g], at_ab(t, s, 0))
        if g == 0:
            loads[0].wait()
            for s in (2, 1, 3):
                choose(auv, s, su.at[s - 1])
                send(su.at[s - 1], uu.at[f], u_s.at[0], u_r.at[s - 1], at_y(s))

    choose(auv, 0, uu.at[f])
    n = iota((T, T), 1)
    chip, y, k = lax.div(n, 64), lax.rem(lax.div(n, 16), 4), lax.rem(lax.div(n, 4), 4)
    source = one_hot(iota((T, T), 0) == ((y * 16 + chip * 2 + c) * 2 + o) * TILES + k)
    langs = jnp.broadcast_to(lang_row[...].astype(jnp.float32), (16, T)).astype(jnp.bfloat16)
    langs = dot(langs, source)[:1]
    m, n = iota((ROWS, T), 0), iota((ROWS, T), 1)
    wanted = (lax.div(m, 4) + o * LANGS).astype(jnp.float32)
    pick[...] = one_hot((langs == wanted) & (lax.rem(n, 4) == lax.rem(m, 4)))

    j, t = iota((ROWS, T), 0), iota((ROWS, T), 1)
    limit = jnp.where(
        t < 2 * TILE,
        jnp.where(t < TILE, live[own], live[own + 1]),
        jnp.where(t < 3 * TILE, live[own + 2], live[own + 3]),
    )
    mask = (lax.div(j, RANK) == lax.div(t, TILE)) & (lax.rem(t, TILE) < limit)
    perm_t = permutation((ROWS, ROWS)).astype(jnp.float32).T.astype(jnp.bfloat16)

    def rows_by_chip(v):
        v = jnp.where(mask, v, 0.0).astype(jnp.bfloat16)
        return dot(perm_t, v).astype(jnp.bfloat16)

    for t in range(2):
        b_sends(t, 0)
    bt = jnp.zeros((ROWS, T), jnp.float32)
    bb = jnp.zeros((T, ROWS), jnp.float32)
    for s in (0, 1, 3, 2):
        y = mod(f - s, 4)
        if s:
            await_ref(uu.at[y], u_r.at[s - 1])
        rows = og[:, pl.ds(pl.multiple_of(y * Q_SH, TILE), Q_SH)]
        bt += dot(uu[y], rows, NT)
        bb += dot(rows, uu[y], NT)
    tt, jj = iota((T, ROWS), 0), iota((T, ROWS), 1)
    bb = jnp.where(lax.div(jj, RANK) == lax.div(tt, TILE), bb, 0.0).astype(jnp.bfloat16)
    b2[...] = (bb.astype(jnp.float32) * 2.0).astype(jnp.bfloat16)
    btp[...] = rows_by_chip(bt)

    loads[3].wait()
    for s in (2, 1, 3, 0):
        y = mod(f + s, 4)
        part = dot(btp[...], tok[:, pl.ds(pl.multiple_of(y * D_SH, TILE), D_SH)]).astype(jnp.bfloat16)
        if s:
            spd[s - 1] = part
            send(spd.at[s - 1], r1d.at[f], pd_s.at[0], pd_r.at[0], at_y(s))
        else:
            r1d[f] = part

    loads[1].wait()
    for s in (2, 1, 3):
        choose(adv, s, sd.at[s - 1])
        send(sd.at[s - 1], dd.at[f], d_s.at[0], d_r.at[s - 1], at_y(s))
    choose(adv, 0, dd.at[f])

    def spread(r1, r2, s, ssem, rsem):
        y = mod(f - s, 4)

        def one(i, _):
            chip = lax.rem(q + i, CHIPS)
            rcopy(
                r1.at[y, pl.ds(pl.multiple_of(chip * 16, 16), 16)], r2.at[q, y],
                ssem, rsem, at_chip(chip),
            ).start()
            return 0

        lax.fori_loop(1, CHIPS, one, 0)
        pltpu.make_async_copy(r1.at[y, pl.ds(pl.multiple_of(q * 16, 16), 16)], r2.at[q, y], rsem).start()

    spread(r1d, r2d, 0, xd_s.at[0], xd_r.at[0])

    for s in (1, 3, 2):
        for t in range(2):
            for g in range(2):
                await_ref(piece(wbuf, groups[g][0], t, mod(pa[t] - s, 4), pb[t]), a_r.at[t, s - 1, g])
            b_sends(t, s)

    def block(t, rel):
        rows = pl.ds(pl.multiple_of(first_row(t, c) + mod(pb[t] + rel, 4) * SUBS[t], 16), SUBS[t])
        return wbuf.at[:, rows]

    def block_to_other(t, rel):
        send(block(t, rel), block(t, rel), w_s.at[0], c_r.at[t], other)

    def block_arrived(t):
        await_ref(block(t, 2), f_r.at[t])

    block_to_other(0, 0)

    def way_of(t, s):
        return (1 - swap[t]) * (2 * lax.rem(z, 2) - 1) + swap[t] * (1 if s in (0, 2) else -1)

    def pass_on(t, s):
        way = way_of(t, s)
        unit = piece(wbuf, every, t, mod(pa[t] - s, 4), mod(pb[t] - way, 4))
        await_ref(unit, b_r.at[t, lax.div(1 - way, 2), s])
        send(unit, unit, w_s.at[0], f_r.at[t], at_ab(t, 0, way))

    def rest(t, s):
        way = way_of(t, s)
        await_ref(piece(wbuf, every, t, mod(pa[t] - s, 4), mod(pb[t] + way, 4)), b_r.at[t, lax.div(1 + way, 2), s])

    pass_on(0, 0)

    def columns(w, y, first, width):
        d = dd[y, :, pl.ds(first, width)]
        value = (dot(og[...], w, NT) + dot(b2[...], d)).astype(jnp.bfloat16)
        ig[:, pl.ds(pl.multiple_of(y * D_SH + first, TILE), width)] = value

    loads[4].wait()

    def local_chunk(i, _):
        first = pl.multiple_of(i * LOCAL, TILE)
        columns(wl[pl.ds(first, LOCAL), :], f, first, LOCAL)
        return 0

    lax.fori_loop(0, D_SH // LOCAL, local_chunk, 0)

    def gathered(i, core):
        first = pl.multiple_of(core * MAIN, TILE)
        columns(wbuf[i, pl.ds(first, MAIN), :], mod(f + SLOTS[i], 4), first, MAIN)

    def spread_down(s):
        spread(r1d, r2d, s, xd_s.at[0], xd_r.at[0])

    def spread_up(s):
        spread(r1u, r2u, s, xu_s.at[0], xu_r.at[0])

    await_ref(r1d.at[pl.ds(0, 3)], pd_r.at[0])
    for s in (1, 3, 2):
        spread_down(s)
    for s in (1, 3, 2):
        pass_on(0, s)
    for s in range(4):
        rest(0, s)
    for rel in (1, 3):
        block_to_other(0, rel)
    ht = jnp.zeros((ROWS, T), jnp.float32)
    for s in (0, 1, 3, 2):
        y = mod(f - s, 4)
        if s:
            await_ref(dd.at[y], d_r.at[s - 1])
        ht += dot(dd[y], tok[:, pl.ds(pl.multiple_of(y * D_SH, TILE), D_SH)], NT)
    htp[...] = rows_by_chip(ht)
    for s in (2, 1, 3, 0):
        y = mod(f + s, 4)
        part = dot(htp[...], og[:, pl.ds(pl.multiple_of(y * Q_SH, TILE), Q_SH)]).astype(jnp.bfloat16)
        if s:
            spu[s - 1] = part
            send(spu.at[s - 1], r1u.at[f], pu_s.at[0], pu_r.at[0], at_y(s))
        else:
            r1u[f] = part
    spread(r1u, r2u, 0, xu_s.at[0], xu_r.at[0])

    def tail_rows(i, late):
        half = (1 - i) * (1 - late) + i * late
        return pl.ds(pl.multiple_of(2 * HALF + c * MINE + half * (MINE // 2), 16), MINE // 2)

    def tail_sends(late):
        for i, s in ((1, 1), (0, 3)):
            rows = tail_rows(i, late)
            send(weight.at[rows], wbuf.at[i, rows], w_s.at[0], t_r.at[i, late], at_y(s))

    tail_sends(0)
    tail_sends(1)

    for s in (0, 1, 3, 2):
        pass_on(1, s)
    block_arrived(0)
    block_to_other(0, 2)

    scale = 2.0 / 256.0

    def send_sum(width):
        part, there = xout.at[:, pl.ds(0, width)], xin.at[:, pl.ds(0, width)]
        return rcopy(part, there, xc_s.at[0], xc_r.at[0], other)

    def place(dz, s, r):
        return gg.at[chip_of(dz, s), :, pl.ds(*PARTS[r])]

    def mine(r):
        return gv.at[:, pl.ds(PARTS[r][0] - (D_SH if r > 1 else 0), PARTS[r][1])]

    def to_x(src, dst, r, k):
        for s in (2, 1, 3):
            rcopy(src, dst, g_s.at[0], g_r.at[r % 2, k + s - 1], at_chip(chip_of(0, -s))).start()

    def to_z(src, dst, r, k):
        rcopy(src, dst, g_s.at[0], g_r.at[r % 2, k], at_chip(chip_of(1, 0))).start()

    def to_core(src, dst, r, k):
        rcopy(src, dst, e_s.at[0], e_r.at[0], other).start()

    def start_gather(r):
        to_z(mine(r + 1), place(0, 0, r + 1), r + 1, 3)
        to_x(mine(r), place(0, 0, r), r, 0)
        to_x(mine(r + 1), place(0, 0, r + 1), r + 1, 0)
        to_z(mine(r), place(0, 0, r), r, 3)
        for h in (r, r + 1):
            to_core(mine(h), place(0, 0, h), h, 0)
            pltpu.make_async_copy(mine(h), place(0, 0, h), own_s.at[0]).start()

    def turn(r):
        part = hand_over(1, 0, r + 1)
        to_x(part, part, r + 1, 4)
        for s in (1, 3, 2):
            part = hand_over(0, s, r)
            to_z(part, part, r, 3 + s)

    def last_hop(r):
        for dz in (0, 1):
            for s in (1, 3, 2):
                hand_over(dz, s, r + 1)
        for s in (0, 1, 3, 2):
            hand_over(1, s, r)

    def hand_over(dz, s, r):
        part = place(dz, s, r)
        await_ref(part, g_r.at[r % 2, s - 1 if dz == 0 else 3 + s])
        to_core(part, part, r, dz * 4 + s)
        return part

    await_ref(r2d, xd_r.at[0])
    down = dot(pick[...], r2d[...].reshape(T, D_SH))

    @pl.when(c == 1)
    def _():
        xout[...] = down
        send_sum(D_SH).start()

    gathered(0, c)
    gathered(1, c)
    await_ref(r1u.at[pl.ds(0, 3)], pu_r.at[0])
    for s in (1, 3, 2):
        spread_up(s)

    @pl.when(c == 0)
    def _():
        await_ref(xin, xc_r.at[0])
        gv[...] = ((down + xin[...]) * scale).astype(jnp.bfloat16)
        start_gather(0)

    gathered(2, c)
    await_ref(r2u, xu_r.at[0])
    up = dot(pick[...], r2u[...].reshape(T, Q_SH))

    @pl.when(c == 0)
    def _():
        xout[:, :Q_SH] = up
        send_sum(Q_SH).start()

    for i, s in ((1, 1), (0, 3)):
        rows = tail_rows(i, 0)
        await_ref(wbuf.at[i, rows], t_r.at[i, 0])
        send(wbuf.at[i, rows], wbuf.at[2, rows], w_s.at[0], tf_r.at[i], at_y(s))

    @pl.when(c == 1)
    def _():
        await_ref(xin.at[:, pl.ds(0, Q_SH)], xc_r.at[0])
        gv[:, :Q_SH] = ((up + xin[:, :Q_SH]) * scale).astype(jnp.bfloat16)
        start_gather(2)

    def from_other(t):
        rows = pl.ds(pl.multiple_of(first_row(t, 1 - c), 16), 4 * SUBS[t])
        await_ref(wbuf.at[:, rows], c_r.at[t])

    from_other(0)
    gathered(0, 1 - c)

    @pl.when(c == 0)
    def _():
        turn(0)

    gathered(1, 1 - c)
    mine_rows = pl.ds(pl.multiple_of(2 * HALF + c * MINE, 16), MINE)
    theirs = pl.ds(pl.multiple_of(2 * HALF + (1 - c) * MINE, 16), MINE)
    for i in range(2):
        await_ref(wbuf.at[i, tail_rows(i, 1)], t_r.at[i, 1])
    near = wbuf.at[pl.ds(0, 2), mine_rows]
    send(near, near, w_s.at[0], tc_r.at[0], other)
    for s in range(4):
        rest(1, s)
    block_arrived(1)
    for rel in range(4):
        block_to_other(1, rel)

    @pl.when(c == 1)
    def _():
        turn(2)

    gathered(2, 1 - c)

    from_other(1)
    await_ref(wbuf.at[pl.ds(0, 2), theirs], tc_r.at[0])
    last = D_SH - 2 * MAIN
    near_sum = dot(og[...], wbuf[0:2, 2 * MAIN :, :].reshape(2 * last, Q_ALL), NT)
    for i in range(2):
        y = mod(f + SLOTS[i], 4)
        value = near_sum[:, i * last : (i + 1) * last] + dot(b2[...], dd[y, :, 2 * MAIN :])
        ig[:, pl.ds(pl.multiple_of(y * D_SH + 2 * MAIN, TILE), last)] = value.astype(jnp.bfloat16)
    for i in range(2):
        await_ref(wbuf.at[2, tail_rows(i, 0)], tf_r.at[i])
    far = wbuf.at[2, mine_rows]
    send(far, far, w_s.at[0], tc_r.at[1], other)

    @pl.when(c == 0)
    def _():
        last_hop(0)

    @pl.when(c == 1)
    def _():
        last_hop(2)

    await_ref(wbuf.at[2, theirs], tc_r.at[1])
    columns(wbuf[2, 2 * MAIN :, :], mod(f + SLOTS[2], 4), 2 * MAIN, last)

    def finish(width, first):
        ours, theirs = pl.ds(first, width), pl.ds(D_SH - first, G_ALL - width)
        await_ref(gg.at[:, :, theirs], e_r.at[0])
        send_sum(G_ALL - width).wait_send()
        await_ref(gv.at[:, pl.ds(0, width)], own_s.at[0])
        await_ref(gg.at[pl.ds(0, CHIPS - 1), :, ours], g_s.at[0])
        await_ref(gg.at[:, :, ours], e_s.at[0])

    @pl.when(c == 0)
    def _():
        finish(D_SH, 0)

    @pl.when(c == 1)
    def _():
        finish(Q_SH, D_SH)

    await_ref(wbuf, w_s.at[0])
    for ref, ssem in ((su, u_s), (sd, d_s), (spd, pd_s), (spu, pu_s)):
        await_ref(ref, ssem.at[0])
    for r1, ssem in ((r1d, xd_s), (r1u, xu_s)):
        await_ref(r1.at[:, pl.ds(0, 16 * (CHIPS - 1))], ssem.at[0])


def finish_kernel(gg, ig_in, down, up, ig, dv, uv, out_s):
    outs = []

    def emit(src, dst, i, g):
        cp = pltpu.make_async_copy(src, dst, out_s.at[i, g])
        cp.start()
        outs.append(cp)

    for g in range(4):
        rows = pl.ds(g * TILE, TILE)
        emit(ig_in.at[rows], ig.at[rows], 2, g)
    perm = permutation((ROWS, ROWS))
    for g in range(4):
        for h in (2 * g, 2 * g + 1):
            rows = gg[:, h * 16 : (h + 1) * 16, :].reshape(ROWS, G_ALL)
            rows = dot(perm, rows).astype(jnp.bfloat16).reshape(4, RANK, G_ALL)
            dv[h * 4 : (h + 1) * 4] = rows[:, :, :D_SH]
            uv[h * 4 : (h + 1) * 4] = rows[:, :, D_SH:]
        part = pl.ds(g * 8, 8)
        emit(dv.at[part], down.at[part], 0, g)
        emit(uv.at[part], up.at[part], 1, g)
    for cp in outs:
        cp.wait()


def on_device(tokens, output_gradient, tile_language, tile_live_count, frozen_weight, adapter_down, adapter_up):
    bf = jnp.bfloat16
    pin = pltpu.with_memory_space_constraint
    tokens, output_gradient, frozen_weight, adapter_down, adapter_up = (
        pin(a, pltpu.HBM) for a in (tokens, output_gradient, frozen_weight, adapter_down, adapter_up)
    )
    hbm, smem, vmem = (pl.BlockSpec(memory_space=s) for s in (pl.ANY, pltpu.SMEM, pltpu.VMEM))
    sem = pltpu.SemaphoreType.DMA

    def sems(*shapes):
        return [sem(s) for s in shapes]

    def buf(*shape, dtype=bf):
        return pltpu.VMEM(shape, dtype)

    ig, gg = pl.pallas_call(
        main_kernel,
        out_shape=(
            buf(T, D_ALL),
            buf(CHIPS, ROWS, G_ALL),
        ),
        in_specs=[smem, smem, vmem, hbm, hbm, hbm, hbm, hbm],
        out_specs=(vmem, vmem),
        scratch_shapes=[
            buf(3, D_SH, Q_ALL),
            buf(D_SH, Q_ALL),
            buf(T, D_ALL),
            buf(T, Q_ALL),
            buf(LANGS, RANK, D_SH),
            buf(LANGS, RANK, Q_SH),
            buf(3, ROWS, Q_SH),
            buf(3, ROWS, D_SH),
            buf(YN, ROWS, Q_SH),
            buf(YN, ROWS, D_SH),
            buf(3, ROWS, D_SH),
            buf(3, ROWS, Q_SH),
            buf(YN, ROWS, D_SH),
            buf(YN, ROWS, Q_SH),
            buf(CHIPS, YN, 16, D_SH),
            buf(CHIPS, YN, 16, Q_SH),
            buf(ROWS, D_SH, dtype=jnp.float32),
            buf(ROWS, D_SH, dtype=jnp.float32),
            buf(ROWS, D_SH),
            buf(T, ROWS),
            buf(ROWS, T),
            buf(ROWS, T),
            buf(ROWS, T),
            *sems((5,), (1,), (2, 3), (2, 3, 2), (2, 2, 4), (2,), (2,), (2, 2), (2,), (2,)),
            *sems((1,), (3,), (1,), (3,), *[(1,)] * 4, *[(1,)] * 4, (1,), (1,), (1,), (2, 7), (1,), (1,), (1,)),
        ],
        compiler_params=pltpu.CompilerParams(
            collective_id=0, has_side_effects=True, vmem_limit_bytes=46 * 2**20
        ),
        cost_estimate=pl.CostEstimate(flops=12 * 10**9, bytes_accessed=40 * 10**6, transcendentals=0),
        name="exchange",
    )(
        pin(tile_language, pltpu.HBM), pin(tile_live_count, pltpu.HBM), tile_language.reshape(1, T),
        tokens, output_gradient, frozen_weight, adapter_down, adapter_up,
    )
    down, up, ig = pl.pallas_call(
        finish_kernel,
        out_shape=(
            jax.ShapeDtypeStruct((LANGS, RANK, D_SH), bf),
            jax.ShapeDtypeStruct((LANGS, RANK, Q_SH), bf),
            jax.ShapeDtypeStruct((T, D_ALL), bf),
        ),
        in_specs=[vmem, vmem],
        out_specs=(hbm, hbm, hbm),
        scratch_shapes=[buf(LANGS, RANK, D_SH), buf(LANGS, RANK, Q_SH), sem((3, 4))],
        compiler_params=pltpu.CompilerParams(vmem_limit_bytes=16 * 2**20),
        name="finish",
    )(pin(gg, pltpu.VMEM), pin(ig, pltpu.VMEM))
    return ig, down, up


def solution(mesh):
    tok = P(("fsdp", "dp", "owner"), None)
    adapter = P("owner", None, "fsdp")
    return jax.shard_map(
        on_device,
        mesh=mesh,
        in_specs=(tok, tok, P(), P(), P("fsdp", None), adapter, adapter),
        out_specs=(tok, adapter, adapter),
        check_vma=False,
    )
```
